32 devices in a mesh: parts: 2 (over x), band: 2 (over core), block: 8 (over z, y).
Axes of the slice: x: 2, y: 2, z: 4, core: 2. Of those that a mesh axis runs over, the one named last changes fastest.
Arguments:
- grid_input: bfloat16 [256, 128, 256], P(('parts', 'band'), 'block'), parts along dimension 0, may hold values from -6 to 6
- grad_output: bfloat16 [256, 128, 256], P(('parts', 'band'), 'block'), parts along dimension 0, may hold values from -6 to 6
- context_tile: int32 [64, 32], P(('parts', 'band'), 'block'), parts along dimension 0, may hold values from 0 to 127
- gains: float32 [2, 256], replicated, may hold values from 0.4 to 1.6
- row_weights: bfloat16 [4, 256, 256], replicated, may hold values from -0.375 to 0.375
- column_weights: bfloat16 [4, 256, 256], replicated, may hold values from -0.375 to 0.375
Outputs:
- grad_input: bfloat16 [256, 128, 256], P(('parts', 'band'), 'block'), parts along dimension 0
- grad_row_weights: float32 [8, 256, 256], P('parts'), parts along dimension 0
- grad_column_weights: float32 [8, 256, 256], P('parts'), parts along dimension 0
- grad_gains: float32 [4, 256], P('parts'), parts along dimension 0
- grad_context: float32 [256, 256], P(('parts', 'band', 'block')), parts along dimension 0
The draws below stay inside these ranges and needn't reach their ends.
There are 2 independent parts, one for each index of `parts`. The reference program is written for one: setup_inputs(seed, part) draws one part's arguments, and reference() takes and returns one part's arrays. A program takes and returns all parts, laid end to end along the dimension named above; an argument that names none is the same for every part. Nothing has to cross between parts.
Inputs may be any that keep to these rules, and one draw needn't show every extreme that they name: `context_tile`: each patch reads one tile.
All inputs are finite; a program needn't handle non-finite values.
Results may differ from the reference program's by a relative error of at most 0.012.
The reference program's roundings to bfloat16 on the way count: a program that leaves them out, or rounds other values in their place, can miss the bound.
Values may be sent and summed in bfloat16 or wider, within the bound.
A program may use at most 64 MiB of HBM per device.

```python
import math
import jax
import jax.numpy as jnp
from jax import lax

HEADS = 8
D = 256
H = 128
W = 128
TILES = 128


def set_ends(values, key, least, high):
    longest = values.shape.index(max(values.shape))
    spots = []
    for shift in (0, 1):
        where = [jax.random.randint(jax.random.fold_in(key, axis), (), 0, length) for axis, length in enumerate(values.shape)]
        where[longest] = (where[longest] + shift) % values.shape[longest]
        spots.append(tuple(where))
    return values.at[spots[0]].set(least).at[spots[1]].set(high)


def levels(own_key, extent, pieces, smallest, high):
    level = 1.0
    for axis_at, parts in pieces:
        draws = jax.random.uniform(jax.random.fold_in(jax.random.fold_in(own_key, 6), axis_at), (parts,), jnp.float32, smallest / len(pieces), high / len(pieces))
        level = level * jnp.repeat(jnp.exp(draws), extent[axis_at] // parts).reshape((-1,) + (1,) * (len(extent) - 1 - axis_at))
    return level


def noise(stream_key, extent, spread, limit, cuts=(), dtype=jnp.bfloat16):
    values = jax.random.normal(stream_key, extent, jnp.float32) * spread
    if len(cuts) > 0:
        values = levels(stream_key, extent, cuts, -0.22, 0.18) * values
    return jnp.clip(values, min=-limit, max=limit).astype(dtype)


def setup_inputs(seed: int = 0, part: int = 0) -> dict:
    key_list = jax.random.split(jax.random.key(seed), 7)
    own_keys = jax.random.split(jax.random.fold_in(key_list[6], part), 7)
    grid_input = noise(own_keys[0], (H, W, D), 1.0, 6.0, ((0, 2), (1, 8)))
    grad_output = noise(own_keys[1], (H, W, D), 1.0, 6.0, ((0, 2), (1, 8)))
    context_tile = set_ends(jax.random.randint(own_keys[2], (H // 4, W // 4), 0, TILES), jax.random.fold_in(own_keys[2], 1), 0, TILES - 1).astype(jnp.int32)
    gains = jnp.clip(1.0 + 0.12 * jax.random.normal(key_list[3], (2, D), jnp.float32), 0.4, 1.6)
    row_weights = noise(key_list[4], (4, D, D), D ** -0.5, 0.375)
    column_weights = noise(key_list[5], (4, D, D), D ** -0.5, 0.375)
    return dict(grid_input=grid_input, grad_output=grad_output, context_tile=context_tile, gains=gains, row_weights=row_weights, column_weights=column_weights)


EPS = 1e-06

def project_in(inputs, gain, weights):
    features = inputs.shape[-1]
    widened = inputs.astype(jnp.float32)
    inverse_rms = lax.rsqrt(lax.optimization_barrier(jnp.mean(widened * widened, axis=-1, keepdims=True)) + EPS)
    unit_rows = widened * inverse_rms
    normed = (unit_rows * gain).astype(jnp.bfloat16)
    stacked = jnp.concatenate([weights[0], weights[1], weights[2]], axis=1)
    projected = jnp.dot(normed.reshape(-1, features), stacked, preferred_element_type=jnp.float32)
    packed = projected.astype(jnp.bfloat16).reshape(inputs.shape[:-1] + (3 * features,))
    return (normed, unit_rows, inverse_rms, packed)

def head_attend(queries, key_rows, values, direction):
    scaling = 1.0 / math.sqrt(queries.shape[-1])
    if direction == 'row':
        scores = jnp.einsum('ald,amd->alm', queries, key_rows, preferred_element_type=jnp.float32)
    else:
        scores = jnp.einsum('lbd,mbd->blm', queries, key_rows, preferred_element_type=jnp.float32)
    soft_weights = jax.nn.softmax(scores * scaling, axis=-1).astype(jnp.bfloat16)
    if direction == 'row':
        result = jnp.einsum('alm,amd->ald', soft_weights, values, preferred_element_type=jnp.float32)
    else:
        result = jnp.einsum('blm,mbd->lbd', soft_weights, values, preferred_element_type=jnp.float32)
    return result.astype(jnp.bfloat16)

def split_heads(packed, head_count):
    features = packed.shape[-1] // 3
    head_size = features // head_count
    portions = []
    for member in range(3):
        portion = packed[..., member * features:(member + 1) * features]
        portion = portion.reshape(packed.shape[:-1] + (head_count, head_size))
        portions.append(jnp.moveaxis(portion, -2, 0))
    return portions

def join_heads(stacked):
    rearranged = jnp.moveaxis(stacked, 0, -2)
    return rearranged.reshape(rearranged.shape[:-2] + (rearranged.shape[-2] * rearranged.shape[-1],))

def attend(packed, head_count, direction):
    queries, key_rows, values = split_heads(packed, head_count)
    results = lax.map(lambda triple: head_attend(triple[0], triple[1], triple[2], direction), (queries, key_rows, values))
    return join_heads(results)

def attend_back(packed, grad_mixed, head_count, direction):
    queries, key_rows, values = split_heads(packed, head_count)
    head_size = queries.shape[-1]
    cotangents = jnp.moveaxis(grad_mixed.reshape(grad_mixed.shape[:-1] + (head_count, head_size)), -2, 0)

    def single_head(quad):
        _, pullback = jax.vjp(lambda first, second, third: head_attend(first, second, third, direction), quad[0], quad[1], quad[2])
        return pullback(quad[3])
    grad_query, grad_key, grad_value = lax.map(single_head, (queries, key_rows, values, cotangents))
    return jnp.concatenate([join_heads(grad_query), join_heads(grad_key), join_heads(grad_value)], axis=-1)

def project_out(inputs, mixed, weight_out):
    features = inputs.shape[-1]
    added = jnp.dot(mixed.reshape(-1, features), weight_out, preferred_element_type=jnp.float32)
    return (inputs.astype(jnp.float32) + added.reshape(inputs.shape)).astype(jnp.bfloat16)

def output_back(mixed, grad_sum, weight_out):
    features = mixed.shape[-1]
    flat_grad = grad_sum.reshape(-1, features)
    grad_mixed = lax.dot_general(flat_grad, weight_out, (((1,), (1,)), ((), ())), preferred_element_type=jnp.float32)
    grad_weight = lax.dot_general(mixed.reshape(-1, features), flat_grad, (((0,), (0,)), ((), ())), preferred_element_type=jnp.float32)
    return (grad_mixed.astype(jnp.bfloat16).reshape(mixed.shape), grad_weight)

def input_back(normed, unit_rows, inverse_rms, grad_packed, gain, weights, grad_sum):
    features = normed.shape[-1]
    stacked = jnp.concatenate([weights[0], weights[1], weights[2]], axis=1)
    flat_packed = grad_packed.reshape(-1, 3 * features)
    grad_normed = lax.dot_general(flat_packed, stacked, (((1,), (1,)), ((), ())), preferred_element_type=jnp.float32)
    grad_normed = grad_normed.reshape(normed.shape)
    grad_stacked = lax.dot_general(normed.reshape(-1, features), flat_packed, (((0,), (0,)), ((), ())), preferred_element_type=jnp.float32)
    grad_gain = lax.optimization_barrier(jnp.sum((unit_rows * grad_normed).reshape(-1, features), axis=0))
    grad_unit = grad_normed * gain
    inner = lax.optimization_barrier(jnp.mean(grad_unit * unit_rows, axis=-1, keepdims=True))
    result = grad_sum.astype(jnp.float32) + inverse_rms * (grad_unit - unit_rows * inner)
    return (result.astype(jnp.bfloat16), grad_stacked, grad_gain)

def stack_grads(grad_stacked, grad_out):
    features = grad_out.shape[0]
    return jnp.stack([grad_stacked[:, :features], grad_stacked[:, features:2 * features], grad_stacked[:, 2 * features:], grad_out])

def to_groups(array):
    return array.reshape(H, W // 16, 16, array.shape[-1]).transpose(1, 0, 2, 3)

def from_groups(array):
    return array.transpose(1, 0, 2, 3).reshape(H, W, array.shape[-1])

def reference(grid_input, grad_output, context_tile, gains, row_weights, column_weights):
    normed_one, unit_one, inverse_one, packed_one = project_in(grid_input, gains[0], row_weights)
    mixed_one = lax.map(lambda row: attend(row[None], HEADS, 'row')[0], packed_one)
    hidden = project_out(grid_input, mixed_one, row_weights[3])
    normed_two, unit_two, inverse_two, packed_two = project_in(hidden, gains[1], column_weights)
    mixed_two = from_groups(lax.map(lambda group: attend(group, HEADS, 'col'), to_groups(packed_two)))
    grad_mixed_two, grad_out_two = output_back(mixed_two, grad_output, column_weights[3])
    grad_packed_two = from_groups(lax.map(lambda pair: attend_back(pair[0], pair[1], HEADS, 'col'), (to_groups(packed_two), to_groups(grad_mixed_two))))
    grad_hidden, grad_stack_two, grad_gain_two = input_back(normed_two, unit_two, inverse_two, grad_packed_two, gains[1], column_weights, grad_output)
    grad_mixed_one, grad_out_one = output_back(mixed_one, grad_hidden, row_weights[3])
    grad_packed_one = lax.map(lambda pair: attend_back(pair[0][None], pair[1][None], HEADS, 'row')[0], (packed_one, grad_mixed_one))
    grad_input, grad_stack_one, grad_gain_one = input_back(normed_one, unit_one, inverse_one, grad_packed_one, gains[0], row_weights, grad_hidden)
    scaling = 1.0 / math.sqrt(H * W)
    grad_row = stack_grads(grad_stack_one, grad_out_one) * scaling
    grad_col = stack_grads(grad_stack_two, grad_out_two) * scaling
    grad_gain = jnp.stack([grad_gain_one, grad_gain_two]) * scaling
    features = grid_input.shape[-1]
    patch_sums = grad_input.astype(jnp.float32).reshape(H // 4, 4, W // 4, 4, features).sum(axis=(1, 3)).reshape(-1, features)
    grad_context = 0.25 * jax.ops.segment_sum(patch_sums, context_tile.reshape(-1), TILES)
    return (grad_input, grad_row, grad_col, grad_gain, grad_context)
```

```python
import functools
import math

import jax
import jax.numpy as jnp
from jax import lax
from jax.experimental import pallas as pl
from jax.experimental.pallas import tpu as pltpu
from jax.sharding import PartitionSpec as P

HEADS = 8
TILE_DEV = 8


EPS = 1e-06


def project_in(inputs, gain, weights):
    features = inputs.shape[-1]
    widened = inputs.astype(jnp.float32)
    inverse_rms = lax.rsqrt(jnp.mean(widened * widened, axis=-1, keepdims=True) + EPS)
    unit_rows = widened * inverse_rms
    normed = (unit_rows * gain).astype(jnp.bfloat16)
    stacked = jnp.concatenate([weights[0], weights[1], weights[2]], axis=1)
    projected = jnp.dot(normed.reshape(-1, features), stacked, preferred_element_type=jnp.float32)
    packed = projected.astype(jnp.bfloat16).reshape(inputs.shape[:-1] + (3 * features,))
    return (normed, unit_rows, inverse_rms, packed)


def head_attend(queries, key_rows, values, direction):
    scaling = 1.0 / math.sqrt(queries.shape[-1])
    if direction == "row":
        scores = jnp.einsum("ald,amd->alm", queries, key_rows, preferred_element_type=jnp.float32)
    else:
        scores = jnp.einsum("lbd,mbd->blm", queries, key_rows, preferred_element_type=jnp.float32)
    soft_weights = jax.nn.softmax(scores * scaling, axis=-1).astype(jnp.bfloat16)
    if direction == "row":
        result = jnp.einsum(
            "alm,amd->ald", soft_weights, values, preferred_element_type=jnp.float32
        )
    else:
        result = jnp.einsum(
            "blm,mbd->lbd", soft_weights, values, preferred_element_type=jnp.float32
        )
    return result.astype(jnp.bfloat16)


def split_heads(packed, head_count):
    features = packed.shape[-1] // 3
    head_size = features // head_count
    portions = []
    for member in range(3):
        portion = packed[..., member * features : (member + 1) * features]
        portion = portion.reshape(packed.shape[:-1] + (head_count, head_size))
        portions.append(jnp.moveaxis(portion, -2, 0))
    return portions


def join_heads(stacked):
    rearranged = jnp.moveaxis(stacked, 0, -2)
    return rearranged.reshape(
        rearranged.shape[:-2] + (rearranged.shape[-2] * rearranged.shape[-1],)
    )


def attend(packed, head_count, direction):
    queries, key_rows, values = split_heads(packed, head_count)
    results = lax.map(
        lambda triple: head_attend(triple[0], triple[1], triple[2], direction),
        (queries, key_rows, values),
    )
    return join_heads(results)


def attend_back(packed, grad_mixed, head_count, direction):
    queries, key_rows, values = split_heads(packed, head_count)
    head_size = queries.shape[-1]
    cotangents = jnp.moveaxis(
        grad_mixed.reshape(grad_mixed.shape[:-1] + (head_count, head_size)), -2, 0
    )

    def single_head(quad):
        _, pullback = jax.vjp(
            lambda first, second, third: head_attend(first, second, third, direction),
            quad[0],
            quad[1],
            quad[2],
        )
        return pullback(quad[3])

    grad_query, grad_key, grad_value = lax.map(single_head, (queries, key_rows, values, cotangents))
    return jnp.concatenate(
        [join_heads(grad_query), join_heads(grad_key), join_heads(grad_value)], axis=-1
    )


def project_out(inputs, mixed, weight_out):
    features = inputs.shape[-1]
    added = jnp.dot(mixed.reshape(-1, features), weight_out, preferred_element_type=jnp.float32)
    return (inputs.astype(jnp.float32) + added.reshape(inputs.shape)).astype(jnp.bfloat16)


def output_back(mixed, grad_sum, weight_out):
    features = mixed.shape[-1]
    flat_grad = grad_sum.reshape(-1, features)
    grad_mixed = lax.dot_general(
        flat_grad, weight_out, (((1,), (1,)), ((), ())), preferred_element_type=jnp.float32
    )
    grad_weight = lax.dot_general(
        mixed.reshape(-1, features),
        flat_grad,
        (((0,), (0,)), ((), ())),
        preferred_element_type=jnp.float32,
    )
    return (grad_mixed.astype(jnp.bfloat16).reshape(mixed.shape), grad_weight)


def input_back(normed, unit_rows, inverse_rms, grad_packed, gain, weights, grad_sum):
    features = normed.shape[-1]
    stacked = jnp.concatenate([weights[0], weights[1], weights[2]], axis=1)
    flat_packed = grad_packed.reshape(-1, 3 * features)
    grad_normed = lax.dot_general(
        flat_packed, stacked, (((1,), (1,)), ((), ())), preferred_element_type=jnp.float32
    )
    grad_normed = grad_normed.reshape(normed.shape)
    grad_stacked = lax.dot_general(
        normed.reshape(-1, features),
        flat_packed,
        (((0,), (0,)), ((), ())),
        preferred_element_type=jnp.float32,
    )
    grad_gain = jnp.sum((unit_rows * grad_normed).reshape(-1, features), axis=0)
    grad_unit = grad_normed * gain
    inner = jnp.mean(grad_unit * unit_rows, axis=-1, keepdims=True)
    result = grad_sum.astype(jnp.float32) + inverse_rms * (grad_unit - unit_rows * inner)
    return (result.astype(jnp.bfloat16), grad_stacked, grad_gain)


def stack_grads(grad_stacked, grad_out):
    features = grad_out.shape[0]
    return jnp.stack(
        [
            grad_stacked[:, :features],
            grad_stacked[:, features : 2 * features],
            grad_stacked[:, 2 * features :],
            grad_out,
        ]
    )


def shards(grid_input, grad_output, context_tile, gains, row_weights, column_weights):
    band_rows, block_cols, features = grid_input.shape
    normed_one, unit_one, inverse_one, packed_one = project_in(grid_input, gains[0], row_weights)
    packed_row = lax.all_to_all(packed_one, "block", split_axis=0, concat_axis=1, tiled=True)
    mixed_row = attend(packed_row, HEADS, "row")
    mixed_one = lax.all_to_all(mixed_row, "block", split_axis=1, concat_axis=0, tiled=True)
    hidden = project_out(grid_input, mixed_one, row_weights[3])
    hidden_col, grad_col = (
        lax.all_to_all(hidden, "band", split_axis=1, concat_axis=0, tiled=True),
        lax.all_to_all(grad_output, "band", split_axis=1, concat_axis=0, tiled=True),
    )
    normed_two, unit_two, inverse_two, packed_two = project_in(hidden_col, gains[1], column_weights)
    mixed_two = attend(packed_two, HEADS, "col")
    grad_mixed_two, grad_out_two = output_back(mixed_two, grad_col, column_weights[3])
    grad_packed_two = attend_back(packed_two, grad_mixed_two, HEADS, "col")
    grad_hidden_col, grad_stack_two, grad_gain_two = input_back(
        normed_two, unit_two, inverse_two, grad_packed_two, gains[1], column_weights, grad_col
    )
    grad_hidden = lax.all_to_all(grad_hidden_col, "band", split_axis=0, concat_axis=1, tiled=True)
    grad_mixed_one, grad_out_one = output_back(mixed_one, grad_hidden, row_weights[3])
    grad_mixed_row = lax.all_to_all(
        grad_mixed_one, "block", split_axis=0, concat_axis=1, tiled=True
    )
    grad_packed_row = attend_back(packed_row, grad_mixed_row, HEADS, "row")
    grad_packed_one = lax.all_to_all(
        grad_packed_row, "block", split_axis=1, concat_axis=0, tiled=True
    )
    grad_input, grad_stack_one, grad_gain_one = input_back(
        normed_one, unit_one, inverse_one, grad_packed_one, gains[0], row_weights, grad_hidden
    )
    row_terms = stack_grads(grad_stack_one, grad_out_one)
    col_terms = stack_grads(grad_stack_two, grad_out_two)
    gain_terms = jnp.stack([grad_gain_one, grad_gain_two])
    row_total, col_total, gain_total = lax.psum(
        (row_terms, col_terms, gain_terms), ("band", "block")
    )
    cell_count = band_rows * lax.axis_size("band") * block_cols * lax.axis_size("block")
    scaling = 1.0 / math.sqrt(cell_count)
    cell_grads = grad_input.reshape(-1, features)
    cell_tiles = jnp.repeat(jnp.repeat(context_tile, 4, axis=0), 4, axis=1).reshape(-1)
    own_rows = TILE_DEV
    columns = lax.iota(jnp.int32, own_rows * lax.axis_size(("band", "block")))
    onehot = (cell_tiles[:, None] == columns[None, :]).astype(jnp.bfloat16)
    summed = lax.dot_general(
        onehot, cell_grads, (((0,), (0,)), ((), ())), preferred_element_type=jnp.float32
    )
    every_tile = lax.psum(0.25 * summed, ("band", "block"))
    grad_context = lax.dynamic_slice_in_dim(
        every_tile, lax.axis_index(("band", "block")) * own_rows, own_rows, 0
    )
    return (
        grad_input,
        row_total * scaling,
        col_total * scaling,
        gain_total * scaling,
        grad_context,
    )


F32 = jnp.float32
BF16 = jnp.bfloat16
D = 256
L = 128
HD = D // HEADS
SCALE = 1.0 / math.sqrt(HD)
NB = 8
ND = 2 * NB
GROUP = 2
CT = TILE_DEV * ND


def fits_fused(mesh):
    return mesh.shape["band"] == 2 and mesh.shape["block"] == NB


def dot_nn(a, b):
    return lax.dot_general(a, b, (((1,), (0,)), ((), ())), preferred_element_type=F32)


def dot_nt(a, b):
    return lax.dot_general(a, b, (((1,), (1,)), ((), ())), preferred_element_type=F32)


def dot_tn(a, b):
    return lax.dot_general(a, b, (((0,), (0,)), ((), ())), preferred_element_type=F32)


def head_stack(a):
    lane = lax.broadcasted_iota(jnp.int32, (1, D), 1)
    wide = a.astype(F32)
    return jnp.concatenate(
        [jnp.where(lane // HD == h, wide, 0.0).astype(BF16) for h in range(HEADS)], axis=0
    )


def side_by_side(a):
    return jnp.concatenate([a[h * L : (h + 1) * L] for h in range(HEADS)], axis=1)


def norm_parts(v):
    inverse = lax.rsqrt(jnp.mean(v * v, axis=-1, keepdims=True) + EPS)
    return v * inverse, inverse


def attn_probs(q, k):
    s = dot_nt(head_stack(k), q) * SCALE
    parts = []
    for h in range(HEADS):
        one = s[h * L : (h + 1) * L]
        e = jnp.exp(one - jnp.max(one, axis=0, keepdims=True))
        parts.append((e * (1.0 / jnp.sum(e, axis=0, keepdims=True))).astype(BF16))
    return jnp.concatenate(parts, axis=0)


def attn_out(p, v):
    return dot_tn(p, head_stack(v)).astype(BF16)


def attn_back(p, q, k, v, do):
    dp = dot_nt(head_stack(v), do)
    parts = []
    for h in range(HEADS):
        w = p[h * L : (h + 1) * L].astype(F32)
        t = dp[h * L : (h + 1) * L]
        t = t - jnp.sum(t * w, axis=0, keepdims=True)
        parts.append((t * w * SCALE).astype(BF16))
    ds = jnp.concatenate(parts, axis=0)
    dq = dot_tn(ds, head_stack(k)).astype(BF16)
    dk = dot_nn(side_by_side(ds), head_stack(q)).astype(BF16)
    dv = dot_nn(side_by_side(p), head_stack(do)).astype(BF16)
    return jnp.concatenate([dq, dk, dv], axis=1)


def norm_back(v, c, dn, gain):
    u, inverse = norm_parts(v)
    du = dn * gain
    inner = jnp.mean(du * u, axis=-1, keepdims=True)
    dv = c + inverse * (du - u * inner)
    return dv, jnp.sum(u * dn, axis=0, keepdims=True)


def fused_kernel(
    scaling,
    x_ref, g_ref, ct_ref, gains_ref, wr_ref, wro_ref, wc_ref, wco_ref,
    gi_ref, gr_ref, gc_ref, gg_ref, ctx_ref,
    xbuf, ctin, flat, gsend, gcol, hsend, hrecv, cols, cots, ghsend, ghrecv,
    nbuf, obuf, qkvbuf, pbuf, dbuf, cbuf, gisend,
    wsend, wrecv, wfull, ctacc, ctrecv, gacc, grecv,
    send_sem, recv_sem,
):
    band, block = lax.axis_index("band"), lax.axis_index("block")
    me = band * NB + block
    mycol = 2 * block + band

    def peer(i):
        other = lax.rem(me + i, ND)
        return other, other // NB, lax.rem(other, NB)

    def remote(phase, src, dst, to, frm, b, k):
        return pltpu.make_async_remote_copy(
            src_ref=src, dst_ref=dst, send_sem=send_sem.at[phase, to],
            recv_sem=recv_sem.at[phase, frm],
            device_id={"band": b, "block": k}, device_id_type=pl.DeviceIdType.MESH,
        )

    def every(fn, count):
        def step(i, _):
            fn(i)
            return 0
        lax.fori_loop(1, count, step, 0)

    def rows64(ref, j):
        return ref.at[pl.ds(pl.multiple_of(j * 64, 64), 64)]

    def rows8(ref, j):
        return ref.at[pl.ds(pl.multiple_of(j * 8, 8), 8)]

    barrier = pltpu.get_barrier_semaphore()

    def greet(i):
        _, b, k = peer(i)
        pl.semaphore_signal(
            barrier, inc=1, device_id={"band": b, "block": k},
            device_id_type=pl.DeviceIdType.MESH,
        )

    every(greet, ND)
    pl.semaphore_wait(barrier, ND - 1)

    def in_copy(to, frm):
        return remote(
            0, x_ref.at[pl.ds(pl.multiple_of(to * 8, 8), 8)],
            xbuf.at[:, pl.ds(pl.multiple_of(frm * 16, 16), 16)], to, frm, band, to,
        )

    def ct_copy(to, frm):
        return remote(1, ct_ref.at[to], ctin.at[frm], to, frm, band, to)

    def ring(i):
        return lax.rem(block + i, NB)

    every(lambda i: in_copy(ring(i), block).start(), NB)
    every(lambda i: ct_copy(ring(i), block).start(), NB)
    xbuf[:, pl.ds(pl.multiple_of(block * 16, 16), 16)] = x_ref[pl.ds(pl.multiple_of(block * 8, 8), 8)]
    ctin[block] = ct_ref[block]

    def spread(t, _):
        wide = g_ref[t].astype(F32)
        base = (t // 8) * 64 + lax.rem(t, 8)
        for half in range(2):
            for lo in range(2):
                flat[lo, pl.ds(base + half * 512, 8, stride=8), :] = wide[
                    half * 8 : half * 8 + 8, lo * L : lo * L + L
                ]
        return 0

    lax.fori_loop(0, 64, spread, 0)
    for lo in range(2):
        gsend[:, lo * L : lo * L + L] = flat[lo].astype(BF16)

    def half512(ref, j):
        return ref.at[pl.ds(pl.multiple_of(j * 512, 512), 512)]

    def g_copy(to, frm):
        return remote(2, half512(gsend, to), half512(gcol, frm), to, frm, to, block)

    other = 1 - band
    g_copy(other, band).start()
    gcol[pl.ds(pl.multiple_of(band * 512, 512), 512)] = gsend[pl.ds(pl.multiple_of(band * 512, 512), 512)]

    every(lambda i: in_copy(block, ring(i)).wait_recv(), NB)

    gain_r = gains_ref[0:1, :]
    gain_c = gains_ref[1:2, :]
    span = GROUP * L

    def row_fwd(t, _):
        at = pl.ds(pl.multiple_of(t * span, span), span)
        v = jnp.concatenate([xbuf[t * GROUP + i] for i in range(GROUP)], axis=0).astype(F32)
        u, _inv = norm_parts(v)
        n = (u * gain_r).astype(BF16)
        qkv = dot_nn(n, wr_ref[...]).astype(BF16)
        outs = []
        for i in range(GROUP):
            own = qkv[i * L : (i + 1) * L]
            p = attn_probs(own[:, :D], own[:, D : 2 * D])
            pbuf[t * GROUP + i] = p
            outs.append(attn_out(p, own[:, 2 * D :]))
        o = jnp.concatenate(outs, axis=0)
        nbuf[at] = n
        obuf[at] = o
        qkvbuf[at] = qkv
        hidden = v + dot_nn(o, wro_ref[...])
        for i in range(GROUP):
            for lo in range(2):
                flat[lo, pl.ds(t * GROUP + i, L, stride=8), :] = hidden[
                    i * L : (i + 1) * L, lo * L : lo * L + L
                ]
        return 0

    lax.fori_loop(0, 8 // GROUP, row_fwd, 0)
    for lo in range(2):
        hsend[:, lo * L : lo * L + L] = flat[lo].astype(BF16)

    def h_send(i):
        o_, b, k = peer(i)
        return remote(3, rows64(hsend, 2 * k + b), rows64(hrecv, me), o_, me, b, k)

    def h_recv(i):
        o_, b, k = peer(i)
        return remote(3, rows64(hsend, mycol), rows64(hrecv, o_), o_, o_, b, k)

    every(lambda i: h_send(i).start(), ND)
    hrecv[pl.ds(pl.multiple_of(me * 64, 64), 64)] = hsend[pl.ds(pl.multiple_of(mycol * 64, 64), 64)]
    g_copy(band, other).wait_recv()
    cots[...] = gcol[...].astype(F32).reshape(ND, 8, 8, D)
    every(lambda i: h_recv(i).wait_recv(), ND)
    cols[...] = hrecv[...].astype(F32).reshape(ND, 8, 8, D)

    gacc[...] = jnp.zeros_like(gacc)

    def col_step(t, _):
        at = pl.ds(pl.multiple_of(1024 + t * span, span), span)
        v = jnp.concatenate([cols[:, t * GROUP + i].reshape(L, D) for i in range(GROUP)], axis=0)
        c = jnp.concatenate([cots[:, t * GROUP + i].reshape(L, D) for i in range(GROUP)], axis=0)
        cb = c.astype(BF16)
        u, _inv = norm_parts(v)
        n = (u * gain_c).astype(BF16)
        qkv = dot_nn(n, wc_ref[...]).astype(BF16)
        do = dot_nt(cb, wco_ref[...]).astype(BF16)
        outs, backs = [], []
        for i in range(GROUP):
            own = qkv[i * L : (i + 1) * L]
            q, k, w = own[:, :D], own[:, D : 2 * D], own[:, 2 * D :]
            p = attn_probs(q, k)
            outs.append(attn_out(p, w))
            backs.append(attn_back(p, q, k, w, do[i * L : (i + 1) * L]))
        dqkv = jnp.concatenate(backs, axis=0)
        nbuf[at] = n
        obuf[at] = jnp.concatenate(outs, axis=0)
        dbuf[at] = dqkv
        cbuf[at] = cb
        dn = dot_nt(dqkv, wc_ref[...])
        dv, ggain = norm_back(v, c, dn, gain_c)
        gacc[1:2, :] += ggain
        for i in range(GROUP):
            cols[:, t * GROUP + i] = dv[i * L : (i + 1) * L].reshape(ND, 8, D)
        return 0

    lax.fori_loop(0, 8 // GROUP, col_step, 0)
    ghsend[...] = cols[...].reshape(1024, D).astype(BF16)

    def gh_send(i):
        o_, b, k = peer(i)
        return remote(4, rows64(ghsend, o_), rows64(ghrecv, mycol), o_, me, b, k)

    def gh_recv(i):
        o_, b, k = peer(i)
        return remote(4, rows64(ghsend, me), rows64(ghrecv, 2 * k + b), o_, o_, b, k)

    every(lambda i: gh_send(i).start(), ND)
    ghrecv[pl.ds(pl.multiple_of(mycol * 64, 64), 64)] = ghsend[pl.ds(pl.multiple_of(me * 64, 64), 64)]

    def weight_grads(start, slot):
        span_all = pl.ds(start, 1024)
        n = nbuf[span_all]
        for m in range(3):
            wsend[slot, m * D : (m + 1) * D] = (
                dot_tn(n, dbuf[span_all, m * D : (m + 1) * D]) * scaling
            ).astype(BF16)
        wsend[slot, 3 * D : 4 * D] = (dot_tn(obuf[span_all], cbuf[span_all]) * scaling).astype(BF16)

    def rs_send(slot, i):
        o_, b, k = peer(i)
        return remote(5 + slot, rows64(wsend.at[slot], o_), wrecv.at[slot, me], o_, me, b, k)

    def rs_recv(slot, i):
        o_, b, k = peer(i)
        return remote(5 + slot, rows64(wsend.at[slot], me), wrecv.at[slot, o_], o_, o_, b, k)

    def ag_send(slot, i):
        o_, b, k = peer(i)
        return remote(7 + slot, rows64(wfull.at[slot], me), rows64(wfull.at[slot], me), o_, me, b, k)

    def ag_recv(slot, i):
        o_, b, k = peer(i)
        return remote(7 + slot, rows64(wfull.at[slot], me), rows64(wfull.at[slot], o_), o_, o_, b, k)

    def reduce_own(slot):
        every(lambda i: rs_recv(slot, i).wait_recv(), ND)
        wrecv[slot, me] = wsend[slot, pl.ds(pl.multiple_of(me * 64, 64), 64)]
        total = wrecv[slot, 0].astype(F32)
        for j in range(1, ND):
            total = total + wrecv[slot, j].astype(F32)
        wfull[slot, pl.ds(pl.multiple_of(me * 64, 64), 64)] = total.astype(BF16)
        every(lambda i: ag_send(slot, i).start(), ND)

    weight_grads(1024, 1)
    every(lambda i: rs_send(1, i).start(), ND)

    every(lambda i: ct_copy(block, ring(i)).wait_recv(), NB)
    tiles = ctin[0]
    for j in range(1, NB):
        tiles = tiles + ctin[j]
    tile_ids = tiles.astype(jnp.int32)
    ctin[0] = tile_ids.astype(F32)

    every(lambda i: gh_recv(i).wait_recv(), ND)
    for lo in range(2):
        flat[lo] = ghrecv[:, lo * L : lo * L + L].astype(F32)

    ctacc[...] = jnp.zeros_like(ctacc)

    def gi_copy(to, frm):
        return remote(
            9, gisend.at[:, pl.ds(pl.multiple_of(to * 16, 16), 16)],
            gi_ref.at[pl.ds(pl.multiple_of(frm * 8, 8), 8)], to, frm, band, to,
        )

    def row_bwd(t, _):
        at = pl.ds(pl.multiple_of(t * span, span), span)
        v = jnp.concatenate([xbuf[t * GROUP + i] for i in range(GROUP)], axis=0).astype(F32)
        c = jnp.concatenate(
            [
                jnp.concatenate(
                    [flat[lo, pl.ds(t * GROUP + i, L, stride=8), :] for lo in range(2)], axis=1
                )
                for i in range(GROUP)
            ],
            axis=0,
        )
        cb = c.astype(BF16)
        do = dot_nt(cb, wro_ref[...]).astype(BF16)
        qkv = qkvbuf[at]
        backs = []
        for i in range(GROUP):
            own = qkv[i * L : (i + 1) * L]
            backs.append(
                attn_back(
                    pbuf[t * GROUP + i], own[:, :D], own[:, D : 2 * D], own[:, 2 * D :],
                    do[i * L : (i + 1) * L],
                )
            )
        dqkv = jnp.concatenate(backs, axis=0)
        dbuf[at] = dqkv
        cbuf[at] = cb
        dn = dot_nt(dqkv, wr_ref[...])
        dv, ggain = norm_back(v, c, dn, gain_r)
        gacc[0:1, :] += ggain
        dvb = dv.astype(BF16)
        which = ctin[0, pl.ds((t * GROUP) // 4, 1), :]
        rows_of = lax.broadcasted_iota(jnp.int32, (CT, L), 0).astype(F32)
        hot = jnp.where(rows_of == which, 1.0, 0.0).astype(BF16)
        for i in range(GROUP):
            gisend[t * GROUP + i] = dvb[i * L : (i + 1) * L]
            ctacc[...] += dot_nn(hot, dvb[i * L : (i + 1) * L])
        return 0

    lax.fori_loop(0, 8 // GROUP, row_bwd, 0)

    weight_grads(0, 0)
    every(lambda i: rs_send(0, i).start(), ND)
    every(lambda i: gi_copy(ring(i), block).start(), NB)
    gi_ref[pl.ds(pl.multiple_of(block * 8, 8), 8)] = gisend[:, pl.ds(pl.multiple_of(block * 16, 16), 16)]

    def cx_send(i):
        o_, b, k = peer(i)
        return remote(10, rows8(ctacc, o_), ctrecv.at[me], o_, me, b, k)

    def cx_recv(i):
        o_, b, k = peer(i)
        return remote(10, rows8(ctacc, me), ctrecv.at[o_], o_, o_, b, k)

    def gg_send(i):
        o_, b, k = peer(i)
        return remote(11, gacc, grecv.at[me], o_, me, b, k)

    def gg_recv(i):
        o_, b, k = peer(i)
        return remote(11, gacc, grecv.at[o_], o_, o_, b, k)

    every(lambda i: cx_send(i).start(), ND)
    every(lambda i: gg_send(i).start(), ND)
    reduce_own(1)
    reduce_own(0)
    ctrecv[me] = ctacc[pl.ds(pl.multiple_of(me * 8, 8), 8)]
    grecv[me] = gacc[...]
    every(lambda i: cx_recv(i).wait_recv(), ND)
    every(lambda i: gg_recv(i).wait_recv(), ND)
    total, gtotal = ctrecv[0], grecv[0]
    for j in range(1, ND):
        total = total + ctrecv[j]
        gtotal = gtotal + grecv[j]
    ctx_ref[...] = 0.25 * total
    gg_ref[...] = gtotal * scaling
    every(lambda i: ag_recv(1, i).wait_recv(), ND)
    gc_ref[...] = wfull[1].astype(F32)
    every(lambda i: ag_recv(0, i).wait_recv(), ND)
    gr_ref[...] = wfull[0].astype(F32)
    every(lambda i: gi_copy(block, ring(i)).wait_recv(), NB)

    every(lambda i: in_copy(ring(i), block).wait_send(), NB)
    every(lambda i: ct_copy(ring(i), block).wait_send(), NB)
    g_copy(other, band).wait_send()
    every(lambda i: h_send(i).wait_send(), ND)
    every(lambda i: gh_send(i).wait_send(), ND)
    for slot in range(2):
        every(lambda i: rs_send(slot, i).wait_send(), ND)
        every(lambda i: ag_send(slot, i).wait_send(), ND)
    every(lambda i: gi_copy(ring(i), block).wait_send(), NB)
    every(lambda i: cx_send(i).wait_send(), ND)
    every(lambda i: gg_send(i).wait_send(), ND)


def fused_shards(grid_input, grad_output, context_tile, gains, row_weights, column_weights):
    cell_count = grid_input.shape[0] * grid_input.shape[1] * ND
    scaling = 1.0 / math.sqrt(cell_count)
    block = lax.axis_index("block")
    cells = jnp.repeat(context_tile.astype(F32), 4, axis=1).reshape(NB, 2, 16)
    lanes = jnp.tile(cells, (1, 1, NB))
    mine = (lax.iota(jnp.int32, L) // 16) == block
    placed = jnp.pad(jnp.where(mine, lanes, 0.0), ((0, 0), (0, 6), (0, 0)))
    wr = jnp.concatenate([row_weights[0], row_weights[1], row_weights[2]], axis=1)
    wc = jnp.concatenate([column_weights[0], column_weights[1], column_weights[2]], axis=1)
    vm = pl.BlockSpec(memory_space=pltpu.VMEM)
    big = lambda n, d=D, t=BF16: pltpu.VMEM((n, d), t)
    outs = pl.pallas_call(
        functools.partial(fused_kernel, scaling),
        out_shape=(
            jax.ShapeDtypeStruct((64, 16, D), BF16),
            jax.ShapeDtypeStruct((1024, D), F32),
            jax.ShapeDtypeStruct((1024, D), F32),
            jax.ShapeDtypeStruct((8, D), F32),
            jax.ShapeDtypeStruct((TILE_DEV, D), F32),
        ),
        in_specs=[vm] * 8,
        out_specs=(vm,) * 5,
        scratch_shapes=[
            pltpu.VMEM((8, L, D), BF16),
            pltpu.VMEM((NB, 8, L), F32),
            pltpu.VMEM((2, 1024, L), F32),
            big(1024), big(1024), big(1024), big(1024),
            pltpu.VMEM((ND, 8, 8, D), F32),
            pltpu.VMEM((ND, 8, 8, D), F32),
            big(1024), big(1024),
            big(2048), big(2048), big(1024, 3 * D),
            pltpu.VMEM((8, HEADS * L, L), BF16),
            big(2048, 3 * D), big(2048),
            pltpu.VMEM((8, L, D), BF16),
            pltpu.VMEM((2, 1024, D), BF16),
            pltpu.VMEM((2, ND, 64, D), BF16),
            pltpu.VMEM((2, 1024, D), BF16),
            big(CT, D, F32),
            pltpu.VMEM((ND, TILE_DEV, D), F32),
            big(8, D, F32),
            pltpu.VMEM((ND, 8, D), F32),
            pltpu.SemaphoreType.DMA((12, ND)),
            pltpu.SemaphoreType.DMA((12, ND)),
        ],
        compiler_params=pltpu.CompilerParams(
            collective_id=0, has_side_effects=True, vmem_limit_bytes=56 * 1024 * 1024
        ),
    )(grid_input, grad_output, placed, gains, wr, row_weights[3], wc, column_weights[3])
    grad_input, grad_row, grad_col, grad_gain, grad_context = outs
    return (
        grad_input,
        grad_row.reshape(4, D, D),
        grad_col.reshape(4, D, D),
        grad_gain[:2],
        grad_context,
    )


def solution(mesh):
    in_specs = (
        P(("parts", "band"), "block", None),
        P(("parts", "band"), "block", None),
        P(("parts", "band"), "block"),
        P(),
        P(),
        P(),
    )
    out_specs = (
        P(("parts", "band"), "block", None),
        P("parts", None, None),
        P("parts", None, None),
        P("parts", None),
        P(("parts", "band", "block"), None),
    )
    chosen = fused_shards if fits_fused(mesh) else shards
    return jax.shard_map(chosen, mesh=mesh, in_specs=in_specs, out_specs=out_specs, check_vma=False)
```

```python
import functools
import math

import jax
import jax.numpy as jnp
from jax import lax
from jax.experimental import pallas as pl
from jax.experimental.pallas import tpu as pltpu
from jax.sharding import PartitionSpec as P

HEADS = 8
TILE_DEV = 8


EPS = 1e-06


def project_in(inputs, gain, weights):
    features = inputs.shape[-1]
    widened = inputs.astype(jnp.float32)
    inverse_rms = lax.rsqrt(jnp.mean(widened * widened, axis=-1, keepdims=True) + EPS)
    unit_rows = widened * inverse_rms
    normed = (unit_rows * gain).astype(jnp.bfloat16)
    stacked = jnp.concatenate([weights[0], weights[1], weights[2]], axis=1)
    projected = jnp.dot(normed.reshape(-1, features), stacked, preferred_element_type=jnp.float32)
    packed = projected.astype(jnp.bfloat16).reshape(inputs.shape[:-1] + (3 * features,))
    return (normed, unit_rows, inverse_rms, packed)


def head_attend(queries, key_rows, values, direction):
    scaling = 1.0 / math.sqrt(queries.shape[-1])
    if direction == "row":
        scores = jnp.einsum("ald,amd->alm", queries, key_rows, preferred_element_type=jnp.float32)
    else:
        scores = jnp.einsum("lbd,mbd->blm", queries, key_rows, preferred_element_type=jnp.float32)
    soft_weights = jax.nn.softmax(scores * scaling, axis=-1).astype(jnp.bfloat16)
    if direction == "row":
        result = jnp.einsum(
            "alm,amd->ald", soft_weights, values, preferred_element_type=jnp.float32
        )
    else:
        result = jnp.einsum(
            "blm,mbd->lbd", soft_weights, values, preferred_element_type=jnp.float32
        )
    return result.astype(jnp.bfloat16)


def split_heads(packed, head_count):
    features = packed.shape[-1] // 3
    head_size = features // head_count
    portions = []
    for member in range(3):
        portion = packed[..., member * features : (member + 1) * features]
        portion = portion.reshape(packed.shape[:-1] + (head_count, head_size))
        portions.append(jnp.moveaxis(portion, -2, 0))
    return portions


def join_heads(stacked):
    rearranged = jnp.moveaxis(stacked, 0, -2)
    return rearranged.reshape(
        rearranged.shape[:-2] + (rearranged.shape[-2] * rearranged.shape[-1],)
    )


def attend(packed, head_count, direction):
    queries, key_rows, values = split_heads(packed, head_count)
    results = lax.map(
        lambda triple: head_attend(triple[0], triple[1], triple[2], direction),
        (queries, key_rows, values),
    )
    return join_heads(results)


def attend_back(packed, grad_mixed, head_count, direction):
    queries, key_rows, values = split_heads(packed, head_count)
    head_size = queries.shape[-1]
    cotangents = jnp.moveaxis(
        grad_mixed.reshape(grad_mixed.shape[:-1] + (head_count, head_size)), -2, 0
    )

    def single_head(quad):
        _, pullback = jax.vjp(
            lambda first, second, third: head_attend(first, second, third, direction),
            quad[0],
            quad[1],
            quad[2],
        )
        return pullback(quad[3])

    grad_query, grad_key, grad_value = lax.map(single_head, (queries, key_rows, values, cotangents))
    return jnp.concatenate(
        [join_heads(grad_query), join_heads(grad_key), join_heads(grad_value)], axis=-1
    )


def project_out(inputs, mixed, weight_out):
    features = inputs.shape[-1]
    added = jnp.dot(mixed.reshape(-1, features), weight_out, preferred_element_type=jnp.float32)
    return (inputs.astype(jnp.float32) + added.reshape(inputs.shape)).astype(jnp.bfloat16)


def output_back(mixed, grad_sum, weight_out):
    features = mixed.shape[-1]
    flat_grad = grad_sum.reshape(-1, features)
    grad_mixed = lax.dot_general(
        flat_grad, weight_out, (((1,), (1,)), ((), ())), preferred_element_type=jnp.float32
    )
    grad_weight = lax.dot_general(
        mixed.reshape(-1, features),
        flat_grad,
        (((0,), (0,)), ((), ())),
        preferred_element_type=jnp.float32,
    )
    return (grad_mixed.astype(jnp.bfloat16).reshape(mixed.shape), grad_weight)


def input_back(normed, unit_rows, inverse_rms, grad_packed, gain, weights, grad_sum):
    features = normed.shape[-1]
    stacked = jnp.concatenate([weights[0], weights[1], weights[2]], axis=1)
    flat_packed = grad_packed.reshape(-1, 3 * features)
    grad_normed = lax.dot_general(
        flat_packed, stacked, (((1,), (1,)), ((), ())), preferred_element_type=jnp.float32
    )
    grad_normed = grad_normed.reshape(normed.shape)
    grad_stacked = lax.dot_general(
        normed.reshape(-1, features),
        flat_packed,
        (((0,), (0,)), ((), ())),
        preferred_element_type=jnp.float32,
    )
    grad_gain = jnp.sum((unit_rows * grad_normed).reshape(-1, features), axis=0)
    grad_unit = grad_normed * gain
    inner = jnp.mean(grad_unit * unit_rows, axis=-1, keepdims=True)
    result = grad_sum.astype(jnp.float32) + inverse_rms * (grad_unit - unit_rows * inner)
    return (result.astype(jnp.bfloat16), grad_stacked, grad_gain)


def stack_grads(grad_stacked, grad_out):
    features = grad_out.shape[0]
    return jnp.stack(
        [
            grad_stacked[:, :features],
            grad_stacked[:, features : 2 * features],
            grad_stacked[:, 2 * features :],
            grad_out,
        ]
    )


def shards(grid_input, grad_output, context_tile, gains, row_weights, column_weights):
    band_rows, block_cols, features = grid_input.shape
    normed_one, unit_one, inverse_one, packed_one = project_in(grid_input, gains[0], row_weights)
    packed_row = lax.all_to_all(packed_one, "block", split_axis=0, concat_axis=1, tiled=True)
    mixed_row = attend(packed_row, HEADS, "row")
    mixed_one = lax.all_to_all(mixed_row, "block", split_axis=1, concat_axis=0, tiled=True)
    hidden = project_out(grid_input, mixed_one, row_weights[3])
    hidden_col, grad_col = (
        lax.all_to_all(hidden, "band", split_axis=1, concat_axis=0, tiled=True),
        lax.all_to_all(grad_output, "band", split_axis=1, concat_axis=0, tiled=True),
    )
    normed_two, unit_two, inverse_two, packed_two = project_in(hidden_col, gains[1], column_weights)
    mixed_two = attend(packed_two, HEADS, "col")
    grad_mixed_two, grad_out_two = output_back(mixed_two, grad_col, column_weights[3])
    grad_packed_two = attend_back(packed_two, grad_mixed_two, HEADS, "col")
    grad_hidden_col, grad_stack_two, grad_gain_two = input_back(
        normed_two, unit_two, inverse_two, grad_packed_two, gains[1], column_weights, grad_col
    )
    grad_hidden = lax.all_to_all(grad_hidden_col, "band", split_axis=0, concat_axis=1, tiled=True)
    grad_mixed_one, grad_out_one = output_back(mixed_one, grad_hidden, row_weights[3])
    grad_mixed_row = lax.all_to_all(
        grad_mixed_one, "block", split_axis=0, concat_axis=1, tiled=True
    )
    grad_packed_row = attend_back(packed_row, grad_mixed_row, HEADS, "row")
    grad_packed_one = lax.all_to_all(
        grad_packed_row, "block", split_axis=1, concat_axis=0, tiled=True
    )
    grad_input, grad_stack_one, grad_gain_one = input_back(
        normed_one, unit_one, inverse_one, grad_packed_one, gains[0], row_weights, grad_hidden
    )
    row_terms = stack_grads(grad_stack_one, grad_out_one)
    col_terms = stack_grads(grad_stack_two, grad_out_two)
    gain_terms = jnp.stack([grad_gain_one, grad_gain_two])
    row_total, col_total, gain_total = lax.psum(
        (row_terms, col_terms, gain_terms), ("band", "block")
    )
    cell_count = band_rows * lax.axis_size("band") * block_cols * lax.axis_size("block")
    scaling = 1.0 / math.sqrt(cell_count)
    cell_grads = grad_input.reshape(-1, features)
    cell_tiles = jnp.repeat(jnp.repeat(context_tile, 4, axis=0), 4, axis=1).reshape(-1)
    own_rows = TILE_DEV
    columns = lax.iota(jnp.int32, own_rows * lax.axis_size(("band", "block")))
    onehot = (cell_tiles[:, None] == columns[None, :]).astype(jnp.bfloat16)
    summed = lax.dot_general(
        onehot, cell_grads, (((0,), (0,)), ((), ())), preferred_element_type=jnp.float32
    )
    every_tile = lax.psum(0.25 * summed, ("band", "block"))
    grad_context = lax.dynamic_slice_in_dim(
        every_tile, lax.axis_index(("band", "block")) * own_rows, own_rows, 0
    )
    return (
        grad_input,
        row_total * scaling,
        col_total * scaling,
        gain_total * scaling,
        grad_context,
    )


F32 = jnp.float32
BF16 = jnp.bfloat16
D = 256
L = 128
HD = D // HEADS
SCALE = 1.0 / math.sqrt(HD)
NB = 8
ND = 2 * NB
GROUP = 2
CT = TILE_DEV * ND


def fits_fused(mesh):
    return mesh.shape["band"] == 2 and mesh.shape["block"] == NB


def dot_nn(a, b):
    return lax.dot_general(a, b, (((1,), (0,)), ((), ())), preferred_element_type=F32)


def dot_nt(a, b):
    return lax.dot_general(a, b, (((1,), (1,)), ((), ())), preferred_element_type=F32)


def dot_tn(a, b):
    return lax.dot_general(a, b, (((0,), (0,)), ((), ())), preferred_element_type=F32)


def head_stack(a):
    lane = lax.broadcasted_iota(jnp.int32, (1, D), 1)
    wide = a.astype(F32)
    return jnp.concatenate(
        [jnp.where(lane // HD == h, wide, 0.0).astype(BF16) for h in range(HEADS)], axis=0
    )


def side_by_side(a):
    return jnp.concatenate([a[h * L : (h + 1) * L] for h in range(HEADS)], axis=1)


def norm_parts(v):
    inverse = lax.rsqrt(jnp.mean(v * v, axis=-1, keepdims=True) + EPS)
    return v * inverse, inverse


def attn_probs(q, k):
    s = dot_nt(head_stack(k), q) * SCALE
    parts = []
    for h in range(HEADS):
        one = s[h * L : (h + 1) * L]
        e = jnp.exp(one - jnp.max(one, axis=0, keepdims=True))
        parts.append((e * (1.0 / jnp.sum(e, axis=0, keepdims=True))).astype(BF16))
    return jnp.concatenate(parts, axis=0)


def attn_out(p, v):
    return dot_tn(p, head_stack(v)).astype(BF16)


def attn_back(p, q, k, v, do):
    dp = dot_nt(head_stack(v), do)
    parts = []
    for h in range(HEADS):
        w = p[h * L : (h + 1) * L].astype(F32)
        t = dp[h * L : (h + 1) * L]
        t = t - jnp.sum(t * w, axis=0, keepdims=True)
        parts.append((t * w * SCALE).astype(BF16))
    ds = jnp.concatenate(parts, axis=0)
    dq = dot_tn(ds, head_stack(k)).astype(BF16)
    dk = dot_nn(side_by_side(ds), head_stack(q)).astype(BF16)
    dv = dot_nn(side_by_side(p), head_stack(do)).astype(BF16)
    return jnp.concatenate([dq, dk, dv], axis=1)


def norm_back(v, c, dn, gain):
    u, inverse = norm_parts(v)
    du = dn * gain
    inner = jnp.mean(du * u, axis=-1, keepdims=True)
    dv = c + inverse * (du - u * inner)
    return dv, jnp.sum(u * dn, axis=0, keepdims=True)


def fused_kernel(
    scaling,
    x_ref, g_ref, ct_ref, gains_ref, rw_ref, cw_ref,
    gi_ref, gr_ref, gc_ref, gg_ref, ctx_ref,
    xbuf, ctin, flat, gsend, gcol, hsend, hrecv, cols, cots, ghsend, ghrecv,
    nbuf, obuf, qkvbuf, pbuf, dbuf, cbuf, gisend,
    wsend, wpair, wred, wrecv, wfull, ctacc, ctpair, ctrecv, gacc, gpair, grecv, wr_ref, wc_ref,
    send_sem, recv_sem,
):
    band, block = lax.axis_index("band"), lax.axis_index("block")
    me = band * NB + block
    mycol = 2 * block + band

    def peer(i):
        other = lax.rem(me + i, ND)
        return other, other // NB, lax.rem(other, NB)

    def remote(phase, src, dst, to, frm, b, k):
        return pltpu.make_async_remote_copy(
            src_ref=src, dst_ref=dst, send_sem=send_sem.at[phase, to],
            recv_sem=recv_sem.at[phase, frm],
            device_id={"band": b, "block": k}, device_id_type=pl.DeviceIdType.MESH,
        )

    def every(fn, count):
        def step(i, _):
            fn(i)
            return 0
        lax.fori_loop(1, count, step, 0)

    def rows64(ref, j):
        return ref.at[pl.ds(pl.multiple_of(j * 64, 64), 64)]

    def rows8(ref, j):
        return ref.at[pl.ds(pl.multiple_of(j * 8, 8), 8)]

    barrier = pltpu.get_barrier_semaphore()

    def greet(i):
        _, b, k = peer(i)
        pl.semaphore_signal(
            barrier, inc=1, device_id={"band": b, "block": k},
            device_id_type=pl.DeviceIdType.MESH,
        )

    every(greet, ND)
    pl.semaphore_wait(barrier, ND - 1)

    def in_copy(t, to, frm):
        return remote(
            t, x_ref.at[pl.ds(to * 8 + t * GROUP, GROUP)],
            xbuf.at[pl.ds(t * GROUP, GROUP), pl.ds(pl.multiple_of(frm * 16, 16), 16)],
            to, frm, band, to,
        )

    def ct_copy(to, frm):
        return remote(4, ct_ref.at[to], ctin.at[frm], to, frm, band, to)

    def ring(i):
        return lax.rem(block + i, NB)

    def groups(fn, least=0, most=8 // GROUP):
        def step(t, _):
            fn(t)
            return 0
        lax.fori_loop(least, most, step, 0)

    groups(lambda t: every(lambda i: in_copy(t, ring(i), block).start(), NB))
    every(lambda i: ct_copy(ring(i), block).start(), NB)
    xbuf[:, pl.ds(pl.multiple_of(block * 16, 16), 16)] = x_ref[pl.ds(pl.multiple_of(block * 8, 8), 8)]
    ctin[block] = ct_ref[block]

    def spread(t, _):
        wide = g_ref[t].astype(F32)
        base = (t // 8) * 64 + lax.rem(t, 8)
        for half in range(2):
            for lo in range(2):
                flat[lo, pl.ds(base + half * 512, 8, stride=8), :] = wide[
                    half * 8 : half * 8 + 8, lo * L : lo * L + L
                ]
        return 0

    lax.fori_loop(0, 64, spread, 0)
    for lo in range(2):
        gsend[:, lo * L : lo * L + L] = flat[lo].astype(BF16)

    def half512(ref, j):
        return ref.at[pl.ds(pl.multiple_of(j * 512, 512), 512)]

    def g_copy(to, frm):
        return remote(5, half512(gsend, to), half512(gcol, frm), to, frm, to, block)

    other = 1 - band
    g_copy(other, band).start()
    gcol[pl.ds(pl.multiple_of(band * 512, 512), 512)] = gsend[pl.ds(pl.multiple_of(band * 512, 512), 512)]

    for m in range(3):
        wr_ref[:, m * D : (m + 1) * D] = rw_ref[m]
        wc_ref[:, m * D : (m + 1) * D] = cw_ref[m]

    gain_r = gains_ref[0:1, :]
    gain_c = gains_ref[1:2, :]
    span = GROUP * L

    def row_fwd(t, _):
        every(lambda i: in_copy(t, block, ring(i)).wait_recv(), NB)
        at = pl.ds(pl.multiple_of(t * span, span), span)
        v = jnp.concatenate([xbuf[t * GROUP + i] for i in range(GROUP)], axis=0).astype(F32)
        u, _inv = norm_parts(v)
        n = (u * gain_r).astype(BF16)
        qkv = dot_nn(n, wr_ref[...]).astype(BF16)
        outs = []
        for i in range(GROUP):
            own = qkv[i * L : (i + 1) * L]
            p = attn_probs(own[:, :D], own[:, D : 2 * D])
            pbuf[t * GROUP + i] = p
            outs.append(attn_out(p, own[:, 2 * D :]))
        o = jnp.concatenate(outs, axis=0)
        nbuf[at] = n
        obuf[at] = o
        qkvbuf[at] = qkv
        hidden = v + dot_nn(o, rw_ref[3])
        for i in range(GROUP):
            for lo in range(2):
                flat[lo, pl.ds(t * GROUP + i, L, stride=8), :] = hidden[
                    i * L : (i + 1) * L, lo * L : lo * L + L
                ]
        return 0

    lax.fori_loop(0, 8 // GROUP, row_fwd, 0)
    for lo in range(2):
        hsend[:, lo * L : lo * L + L] = flat[lo].astype(BF16)

    def part32(ref, j, u):
        return ref.at[pl.ds(pl.multiple_of(j * 64 + u * 32, 32), 32)]

    def h_send(u, i):
        o_, b, k = peer(i)
        return remote(6 + u, part32(hsend, 2 * k + b, u), part32(hrecv, me, u), o_, me, b, k)

    def h_recv(u, i):
        o_, b, k = peer(i)
        return remote(6 + u, part32(hsend, mycol, u), part32(hrecv, o_, u), o_, o_, b, k)

    groups(lambda u: every(lambda i: h_send(u, i).start(), ND), 0, 2)
    hrecv[pl.ds(pl.multiple_of(me * 64, 64), 64)] = hsend[pl.ds(pl.multiple_of(mycol * 64, 64), 64)]
    g_copy(band, other).wait_recv()
    cots[...] = gcol[...].astype(F32).reshape(ND, 8, 8, D)

    gacc[...] = jnp.zeros_like(gacc)

    def col_step(t, _):
        at = pl.ds(pl.multiple_of(1024 + t * span, span), span)
        v = jnp.concatenate([cols[:, t * GROUP + i].reshape(L, D) for i in range(GROUP)], axis=0)
        c = jnp.concatenate([cots[:, t * GROUP + i].reshape(L, D) for i in range(GROUP)], axis=0)
        cb = c.astype(BF16)
        u, _inv = norm_parts(v)
        n = (u * gain_c).astype(BF16)
        qkv = dot_nn(n, wc_ref[...]).astype(BF16)
        do = dot_nt(cb, cw_ref[3]).astype(BF16)
        outs, backs = [], []
        for i in range(GROUP):
            own = qkv[i * L : (i + 1) * L]
            q, k, w = own[:, :D], own[:, D : 2 * D], own[:, 2 * D :]
            p = attn_probs(q, k)
            outs.append(attn_out(p, w))
            backs.append(attn_back(p, q, k, w, do[i * L : (i + 1) * L]))
        dqkv = jnp.concatenate(backs, axis=0)
        nbuf[at] = n
        obuf[at] = jnp.concatenate(outs, axis=0)
        dbuf[at] = dqkv
        cbuf[at] = cb
        dn = dot_nt(dqkv, wc_ref[...])
        dv, ggain = norm_back(v, c, dn, gain_c)
        gacc[2:3, :] += ggain[:, :L]
        gacc[3:4, :] += ggain[:, L:]
        for i in range(GROUP):
            cols[:, t * GROUP + i] = dv[i * L : (i + 1) * L].reshape(ND, 8, D)
        return 0

    def gh_send(u, i):
        o_, b, k = peer(i)
        return remote(8 + u, part32(ghsend, o_, u), part32(ghrecv, mycol, u), o_, me, b, k)

    def gh_recv(u, i):
        o_, b, k = peer(i)
        return remote(8 + u, part32(ghsend, me, u), part32(ghrecv, 2 * k + b, u), o_, o_, b, k)

    def col_half(u):
        every(lambda i: h_recv(u, i).wait_recv(), ND)

        def take(j, _):
            at = pl.ds(pl.multiple_of(j * 64 + u * 32, 32), 32)
            cols[j, pl.ds(u * 4, 4)] = hrecv[at].astype(F32).reshape(4, 8, D)
            return 0

        lax.fori_loop(0, ND, take, 0)
        lax.fori_loop(u * (4 // GROUP), (u + 1) * (4 // GROUP), col_step, 0)

        def give(j, _):
            at = pl.ds(pl.multiple_of(j * 64 + u * 32, 32), 32)
            ghsend[at] = cols[j, pl.ds(u * 4, 4)].reshape(32, D).astype(BF16)
            return 0

        lax.fori_loop(0, ND, give, 0)
        every(lambda i: gh_send(u, i).start(), ND)

    groups(col_half, 0, 2)
    ghrecv[pl.ds(pl.multiple_of(mycol * 64, 64), 64)] = ghsend[pl.ds(pl.multiple_of(me * 64, 64), 64)]

    def weight_grads(start, slot):
        span_all = pl.ds(start, 1024)
        n = nbuf[span_all]
        for m in range(3):
            wsend[slot, m * D : (m + 1) * D] = (
                dot_tn(n, dbuf[span_all, m * D : (m + 1) * D]) * scaling
            ).astype(BF16)
        wsend[slot, 3 * D : 4 * D] = (dot_tn(obuf[span_all], cbuf[span_all]) * scaling).astype(BF16)

    def pair_copy(slot, to, frm):
        return remote(14 + slot, half512(wsend.at[slot], to), wpair.at[slot], to, frm, to, block)

    def back_copy(slot, to, frm):
        return remote(
            16 + slot, half512(wfull.at[slot], frm), half512(wfull.at[slot], frm), to, frm, to, block
        )

    def rs_copy(slot, to, frm):
        return remote(10 + slot, rows64(wred.at[slot], to), wrecv.at[slot, frm], to, frm, band, to)

    def ag_copy(slot, to, frm):
        own = rows64(wfull.at[slot], band * NB + frm)
        return remote(12 + slot, own, own, to, frm, band, to)

    def reduce_pair(slot):
        pair_copy(slot, band, other).wait_recv()
        own = wsend[slot, pl.ds(pl.multiple_of(band * 512, 512), 512)].astype(F32)
        wred[slot] = (own + wpair[slot].astype(F32)).astype(BF16)
        every(lambda i: rs_copy(slot, ring(i), block).start(), NB)

    def reduce_own(slot):
        wrecv[slot, block] = wred[slot, pl.ds(pl.multiple_of(block * 64, 64), 64)]
        every(lambda i: rs_copy(slot, block, ring(i)).wait_recv(), NB)
        total = wrecv[slot, 0].astype(F32)
        for j in range(1, NB):
            total = total + wrecv[slot, j].astype(F32)
        wfull[slot, pl.ds(pl.multiple_of(me * 64, 64), 64)] = total.astype(BF16)
        every(lambda i: ag_copy(slot, ring(i), block).start(), NB)

    def gather_back(slot):
        every(lambda i: ag_copy(slot, block, ring(i)).wait_recv(), NB)
        back_copy(slot, other, band).start()

    weight_grads(1024, 1)
    pair_copy(1, other, band).start()

    every(lambda i: ct_copy(block, ring(i)).wait_recv(), NB)
    tiles = ctin[0]
    for j in range(1, NB):
        tiles = tiles + ctin[j]
    tile_ids = tiles.astype(jnp.int32)
    ctin[0] = tile_ids.astype(F32)

    groups(lambda u: every(lambda i: gh_recv(u, i).wait_recv(), ND), 0, 2)
    reduce_pair(1)
    for lo in range(2):
        flat[lo] = ghrecv[:, lo * L : lo * L + L].astype(F32)

    ctacc[...] = jnp.zeros_like(ctacc)

    def gi_copy(t, to, frm):
        return remote(
            18 + t,
            gisend.at[pl.ds(t * GROUP, GROUP), pl.ds(pl.multiple_of(to * 16, 16), 16)],
            gi_ref.at[pl.ds(frm * 8 + t * GROUP, GROUP)], to, frm, band, to,
        )

    def row_bwd(t, _):
        at = pl.ds(pl.multiple_of(t * span, span), span)
        v = jnp.concatenate([xbuf[t * GROUP + i] for i in range(GROUP)], axis=0).astype(F32)
        c = jnp.concatenate(
            [
                jnp.concatenate(
                    [flat[lo, pl.ds(t * GROUP + i, L, stride=8), :] for lo in range(2)], axis=1
                )
                for i in range(GROUP)
            ],
            axis=0,
        )
        cb = c.astype(BF16)
        do = dot_nt(cb, rw_ref[3]).astype(BF16)
        qkv = qkvbuf[at]
        backs = []
        for i in range(GROUP):
            own = qkv[i * L : (i + 1) * L]
            backs.append(
                attn_back(
                    pbuf[t * GROUP + i], own[:, :D], own[:, D : 2 * D], own[:, 2 * D :],
                    do[i * L : (i + 1) * L],
                )
            )
        dqkv = jnp.concatenate(backs, axis=0)
        dbuf[at] = dqkv
        cbuf[at] = cb
        dn = dot_nt(dqkv, wr_ref[...])
        dv, ggain = norm_back(v, c, dn, gain_r)
        gacc[0:1, :] += ggain[:, :L]
        gacc[1:2, :] += ggain[:, L:]
        dvb = dv.astype(BF16)
        which = ctin[0, pl.ds((t * GROUP) // 4, 1), :]
        rows_of = lax.broadcasted_iota(jnp.int32, (CT, L), 0).astype(F32)
        hot = jnp.where(rows_of == which, 1.0, 0.0).astype(BF16)
        for i in range(GROUP):
            gisend[t * GROUP + i] = dvb[i * L : (i + 1) * L]
            ctacc[...] += dot_nn(hot, dvb[i * L : (i + 1) * L])
        every(lambda i: gi_copy(t, ring(i), block).start(), NB)
        return 0

    lax.fori_loop(0, 8 // GROUP, row_bwd, 0)

    weight_grads(0, 0)
    pair_copy(0, other, band).start()

    def half64(ref, j):
        return ref.at[pl.ds(pl.multiple_of(j * 64, 64), 64)]

    def cx_pair(to, frm):
        return remote(24, half64(ctacc, to), ctpair, to, frm, to, block)

    def cx_copy(to, frm):
        return remote(22, rows8(ctacc, band * NB + to), ctrecv.at[frm], to, frm, band, to)

    def gg_pair(to, frm):
        return remote(25, gacc, gpair, to, frm, to, block)

    def gg_copy(to, frm):
        return remote(23, gpair, grecv.at[frm], to, frm, band, to)

    cx_pair(other, band).start()
    gg_pair(other, band).start()
    reduce_pair(0)
    reduce_own(1)
    gi_ref[pl.ds(pl.multiple_of(block * 8, 8), 8)] = gisend[:, pl.ds(pl.multiple_of(block * 16, 16), 16)]
    cx_pair(band, other).wait_recv()
    mine64 = pl.ds(pl.multiple_of(band * 64, 64), 64)
    ctacc[mine64] = ctacc[mine64] + ctpair[...]
    gg_pair(band, other).wait_recv()
    gpair[...] = gpair[...] + gacc[...]
    every(lambda i: cx_copy(ring(i), block).start(), NB)
    every(lambda i: gg_copy(ring(i), block).start(), NB)
    ctrecv[block] = ctacc[pl.ds(pl.multiple_of(me * 8, 8), 8)]
    grecv[block] = gpair[...]
    reduce_own(0)
    gather_back(1)
    every(lambda i: cx_copy(block, ring(i)).wait_recv(), NB)
    every(lambda i: gg_copy(block, ring(i)).wait_recv(), NB)
    total, gtotal = ctrecv[0], grecv[0]
    for j in range(1, NB):
        total = total + ctrecv[j]
        gtotal = gtotal + grecv[j]
    ctx_ref[...] = 0.25 * total
    gtotal = gtotal * scaling
    for m in range(2):
        gg_ref[m : m + 1, :] = jnp.concatenate([gtotal[2 * m : 2 * m + 1], gtotal[2 * m + 1 : 2 * m + 2]], axis=1)
    back_copy(1, band, other).wait_recv()
    gc_ref[...] = wfull[1].astype(F32).reshape(4, D, D)
    gather_back(0)
    groups(lambda t: every(lambda i: gi_copy(t, block, ring(i)).wait_recv(), NB))
    back_copy(0, band, other).wait_recv()
    gr_ref[...] = wfull[0].astype(F32).reshape(4, D, D)

    groups(lambda t: every(lambda i: in_copy(t, ring(i), block).wait_send(), NB))
    every(lambda i: ct_copy(ring(i), block).wait_send(), NB)
    g_copy(other, band).wait_send()
    groups(lambda u: every(lambda i: h_send(u, i).wait_send(), ND), 0, 2)
    groups(lambda u: every(lambda i: gh_send(u, i).wait_send(), ND), 0, 2)
    for slot in range(2):
        pair_copy(slot, other, band).wait_send()
        back_copy(slot, other, band).wait_send()
        every(lambda i: rs_copy(slot, ring(i), block).wait_send(), NB)
        every(lambda i: ag_copy(slot, ring(i), block).wait_send(), NB)
    groups(lambda t: every(lambda i: gi_copy(t, ring(i), block).wait_send(), NB))
    cx_pair(other, band).wait_send()
    gg_pair(other, band).wait_send()
    every(lambda i: cx_copy(ring(i), block).wait_send(), NB)
    every(lambda i: gg_copy(ring(i), block).wait_send(), NB)


def fused_shards(grid_input, grad_output, context_tile, gains, row_weights, column_weights):
    cell_count = grid_input.shape[0] * grid_input.shape[1] * ND
    scaling = 1.0 / math.sqrt(cell_count)
    block = lax.axis_index("block")
    cells = jnp.repeat(context_tile.astype(F32), 4, axis=1).reshape(NB, 2, 16)
    lanes = jnp.tile(cells, (1, 1, NB))
    mine = (lax.iota(jnp.int32, L) // 16) == block
    placed = jnp.pad(jnp.where(mine, lanes, 0.0), ((0, 0), (0, 6), (0, 0)))
    vm = pl.BlockSpec(memory_space=pltpu.VMEM)
    big = lambda n, d=D, t=BF16: pltpu.VMEM((n, d), t)
    outs = pl.pallas_call(
        functools.partial(fused_kernel, scaling),
        out_shape=(
            jax.ShapeDtypeStruct((64, 16, D), BF16),
            jax.ShapeDtypeStruct((4, D, D), F32),
            jax.ShapeDtypeStruct((4, D, D), F32),
            jax.ShapeDtypeStruct((2, D), F32),
            jax.ShapeDtypeStruct((TILE_DEV, D), F32),
        ),
        in_specs=[vm] * 6,
        out_specs=(vm,) * 5,
        scratch_shapes=[
            pltpu.VMEM((8, L, D), BF16),
            pltpu.VMEM((NB, 8, L), F32),
            pltpu.VMEM((2, 1024, L), F32),
            big(1024), big(1024), big(1024), big(1024),
            pltpu.VMEM((ND, 8, 8, D), F32),
            pltpu.VMEM((ND, 8, 8, D), F32),
            big(1024), big(1024),
            big(2048), big(2048), big(1024, 3 * D),
            pltpu.VMEM((8, HEADS * L, L), BF16),
            big(2048, 3 * D), big(2048),
            pltpu.VMEM((8, L, D), BF16),
            pltpu.VMEM((2, 1024, D), BF16),
            pltpu.VMEM((2, 512, D), BF16),
            pltpu.VMEM((2, 512, D), BF16),
            pltpu.VMEM((2, NB, 64, D), BF16),
            pltpu.VMEM((2, 1024, D), BF16),
            big(CT, D, F32),
            big(64, D, F32),
            pltpu.VMEM((NB, TILE_DEV, D), F32),
            big(8, L, F32),
            big(8, L, F32),
            pltpu.VMEM((NB, 8, L), F32),
            big(D, 3 * D), big(D, 3 * D),
            pltpu.SemaphoreType.DMA((26, ND)),
            pltpu.SemaphoreType.DMA((26, ND)),
        ],
        compiler_params=pltpu.CompilerParams(
            collective_id=0, has_side_effects=True, vmem_limit_bytes=56 * 1024 * 1024
        ),
    )(grid_input, grad_output, placed, gains, row_weights, column_weights)
    return outs


def solution(mesh):
    in_specs = (
        P(("parts", "band"), "block", None),
        P(("parts", "band"), "block", None),
        P(("parts", "band"), "block"),
        P(),
        P(),
        P(),
    )
    out_specs = (
        P(("parts", "band"), "block", None),
        P("parts", None, None),
        P("parts", None, None),
        P("parts", None),
        P(("parts", "band", "block"), None),
    )
    chosen = fused_shards if fits_fused(mesh) else shards
    return jax.shard_map(chosen, mesh=mesh, in_specs=in_specs, out_specs=out_specs, check_vma=False)
```

```python
import functools
import math

import jax
import jax.numpy as jnp
from jax import lax
from jax.experimental import pallas as pl
from jax.experimental.pallas import tpu as pltpu
from jax.sharding import PartitionSpec as P

HEADS = 8
TILE_DEV = 8


EPS = 1e-06


def project_in(inputs, gain, weights):
    features = inputs.shape[-1]
    widened = inputs.astype(jnp.float32)
    inverse_rms = lax.rsqrt(jnp.mean(widened * widened, axis=-1, keepdims=True) + EPS)
    unit_rows = widened * inverse_rms
    normed = (unit_rows * gain).astype(jnp.bfloat16)
    stacked = jnp.concatenate([weights[0], weights[1], weights[2]], axis=1)
    projected = jnp.dot(normed.reshape(-1, features), stacked, preferred_element_type=jnp.float32)
    packed = projected.astype(jnp.bfloat16).reshape(inputs.shape[:-1] + (3 * features,))
    return (normed, unit_rows, inverse_rms, packed)


def head_attend(queries, key_rows, values, direction):
    scaling = 1.0 / math.sqrt(queries.shape[-1])
    if direction == "row":
        scores = jnp.einsum("ald,amd->alm", queries, key_rows, preferred_element_type=jnp.float32)
    else:
        scores = jnp.einsum("lbd,mbd->blm", queries, key_rows, preferred_element_type=jnp.float32)
    soft_weights = jax.nn.softmax(scores * scaling, axis=-1).astype(jnp.bfloat16)
    if direction == "row":
        result = jnp.einsum(
            "alm,amd->ald", soft_weights, values, preferred_element_type=jnp.float32
        )
    else:
        result = jnp.einsum(
            "blm,mbd->lbd", soft_weights, values, preferred_element_type=jnp.float32
        )
    return result.astype(jnp.bfloat16)


def split_heads(packed, head_count):
    features = packed.shape[-1] // 3
    head_size = features // head_count
    portions = []
    for member in range(3):
        portion = packed[..., member * features : (member + 1) * features]
        portion = portion.reshape(packed.shape[:-1] + (head_count, head_size))
        portions.append(jnp.moveaxis(portion, -2, 0))
    return portions


def join_heads(stacked):
    rearranged = jnp.moveaxis(stacked, 0, -2)
    return rearranged.reshape(
        rearranged.shape[:-2] + (rearranged.shape[-2] * rearranged.shape[-1],)
    )


def attend(packed, head_count, direction):
    queries, key_rows, values = split_heads(packed, head_count)
    results = lax.map(
        lambda triple: head_attend(triple[0], triple[1], triple[2], direction),
        (queries, key_rows, values),
    )
    return join_heads(results)


def attend_back(packed, grad_mixed, head_count, direction):
    queries, key_rows, values = split_heads(packed, head_count)
    head_size = queries.shape[-1]
    cotangents = jnp.moveaxis(
        grad_mixed.reshape(grad_mixed.shape[:-1] + (head_count, head_size)), -2, 0
    )

    def single_head(quad):
        _, pullback = jax.vjp(
            lambda first, second, third: head_attend(first, second, third, direction),
            quad[0],
            quad[1],
            quad[2],
        )
        return pullback(quad[3])

    grad_query, grad_key, grad_value = lax.map(single_head, (queries, key_rows, values, cotangents))
    return jnp.concatenate(
        [join_heads(grad_query), join_heads(grad_key), join_heads(grad_value)], axis=-1
    )


def project_out(inputs, mixed, weight_out):
    features = inputs.shape[-1]
    added = jnp.dot(mixed.reshape(-1, features), weight_out, preferred_element_type=jnp.float32)
    return (inputs.astype(jnp.float32) + added.reshape(inputs.shape)).astype(jnp.bfloat16)


def output_back(mixed, grad_sum, weight_out):
    features = mixed.shape[-1]
    flat_grad = grad_sum.reshape(-1, features)
    grad_mixed = lax.dot_general(
        flat_grad, weight_out, (((1,), (1,)), ((), ())), preferred_element_type=jnp.float32
    )
    grad_weight = lax.dot_general(
        mixed.reshape(-1, features),
        flat_grad,
        (((0,), (0,)), ((), ())),
        preferred_element_type=jnp.float32,
    )
    return (grad_mixed.astype(jnp.bfloat16).reshape(mixed.shape), grad_weight)


def input_back(normed, unit_rows, inverse_rms, grad_packed, gain, weights, grad_sum):
    features = normed.shape[-1]
    stacked = jnp.concatenate([weights[0], weights[1], weights[2]], axis=1)
    flat_packed = grad_packed.reshape(-1, 3 * features)
    grad_normed = lax.dot_general(
        flat_packed, stacked, (((1,), (1,)), ((), ())), preferred_element_type=jnp.float32
    )
    grad_normed = grad_normed.reshape(normed.shape)
    grad_stacked = lax.dot_general(
        normed.reshape(-1, features),
        flat_packed,
        (((0,), (0,)), ((), ())),
        preferred_element_type=jnp.float32,
    )
    grad_gain = jnp.sum((unit_rows * grad_normed).reshape(-1, features), axis=0)
    grad_unit = grad_normed * gain
    inner = jnp.mean(grad_unit * unit_rows, axis=-1, keepdims=True)
    result = grad_sum.astype(jnp.float32) + inverse_rms * (grad_unit - unit_rows * inner)
    return (result.astype(jnp.bfloat16), grad_stacked, grad_gain)


def stack_grads(grad_stacked, grad_out):
    features = grad_out.shape[0]
    return jnp.stack(
        [
            grad_stacked[:, :features],
            grad_stacked[:, features : 2 * features],
            grad_stacked[:, 2 * features :],
            grad_out,
        ]
    )


def shards(grid_input, grad_output, context_tile, gains, row_weights, column_weights):
    band_rows, block_cols, features = grid_input.shape
    normed_one, unit_one, inverse_one, packed_one = project_in(grid_input, gains[0], row_weights)
    packed_row = lax.all_to_all(packed_one, "block", split_axis=0, concat_axis=1, tiled=True)
    mixed_row = attend(packed_row, HEADS, "row")
    mixed_one = lax.all_to_all(mixed_row, "block", split_axis=1, concat_axis=0, tiled=True)
    hidden = project_out(grid_input, mixed_one, row_weights[3])
    hidden_col, grad_col = (
        lax.all_to_all(hidden, "band", split_axis=1, concat_axis=0, tiled=True),
        lax.all_to_all(grad_output, "band", split_axis=1, concat_axis=0, tiled=True),
    )
    normed_two, unit_two, inverse_two, packed_two = project_in(hidden_col, gains[1], column_weights)
    mixed_two = attend(packed_two, HEADS, "col")
    grad_mixed_two, grad_out_two = output_back(mixed_two, grad_col, column_weights[3])
    grad_packed_two = attend_back(packed_two, grad_mixed_two, HEADS, "col")
    grad_hidden_col, grad_stack_two, grad_gain_two = input_back(
        normed_two, unit_two, inverse_two, grad_packed_two, gains[1], column_weights, grad_col
    )
    grad_hidden = lax.all_to_all(grad_hidden_col, "band", split_axis=0, concat_axis=1, tiled=True)
    grad_mixed_one, grad_out_one = output_back(mixed_one, grad_hidden, row_weights[3])
    grad_mixed_row = lax.all_to_all(
        grad_mixed_one, "block", split_axis=0, concat_axis=1, tiled=True
    )
    grad_packed_row = attend_back(packed_row, grad_mixed_row, HEADS, "row")
    grad_packed_one = lax.all_to_all(
        grad_packed_row, "block", split_axis=1, concat_axis=0, tiled=True
    )
    grad_input, grad_stack_one, grad_gain_one = input_back(
        normed_one, unit_one, inverse_one, grad_packed_one, gains[0], row_weights, grad_hidden
    )
    row_terms = stack_grads(grad_stack_one, grad_out_one)
    col_terms = stack_grads(grad_stack_two, grad_out_two)
    gain_terms = jnp.stack([grad_gain_one, grad_gain_two])
    row_total, col_total, gain_total = lax.psum(
        (row_terms, col_terms, gain_terms), ("band", "block")
    )
    cell_count = band_rows * lax.axis_size("band") * block_cols * lax.axis_size("block")
    scaling = 1.0 / math.sqrt(cell_count)
    cell_grads = grad_input.reshape(-1, features)
    cell_tiles = jnp.repeat(jnp.repeat(context_tile, 4, axis=0), 4, axis=1).reshape(-1)
    own_rows = TILE_DEV
    columns = lax.iota(jnp.int32, own_rows * lax.axis_size(("band", "block")))
    onehot = (cell_tiles[:, None] == columns[None, :]).astype(jnp.bfloat16)
    summed = lax.dot_general(
        onehot, cell_grads, (((0,), (0,)), ((), ())), preferred_element_type=jnp.float32
    )
    every_tile = lax.psum(0.25 * summed, ("band", "block"))
    grad_context = lax.dynamic_slice_in_dim(
        every_tile, lax.axis_index(("band", "block")) * own_rows, own_rows, 0
    )
    return (
        grad_input,
        row_total * scaling,
        col_total * scaling,
        gain_total * scaling,
        grad_context,
    )


F32 = jnp.float32
BF16 = jnp.bfloat16
D = 256
L = 128
HD = D // HEADS
SCALE = 1.0 / math.sqrt(HD)
NB = 8
ND = 2 * NB
GROUP = 2
CT = TILE_DEV * ND


def fits_fused(mesh):
    return mesh.shape["band"] == 2 and mesh.shape["block"] == NB


def dot_nn(a, b):
    return lax.dot_general(a, b, (((1,), (0,)), ((), ())), preferred_element_type=F32)


def dot_nt(a, b):
    return lax.dot_general(a, b, (((1,), (1,)), ((), ())), preferred_element_type=F32)


def dot_tn(a, b):
    return lax.dot_general(a, b, (((0,), (0,)), ((), ())), preferred_element_type=F32)


def head_stack(a):
    lane = lax.broadcasted_iota(jnp.int32, (1, D), 1)
    wide = a.astype(F32)
    return jnp.concatenate(
        [jnp.where(lane // HD == h, wide, 0.0).astype(BF16) for h in range(HEADS)], axis=0
    )


def side_by_side(a):
    return jnp.concatenate([a[h * L : (h + 1) * L] for h in range(HEADS)], axis=1)


def norm_parts(v):
    inverse = lax.rsqrt(jnp.mean(v * v, axis=-1, keepdims=True) + EPS)
    return v * inverse, inverse


def attn_probs(q, k):
    s = dot_nt(head_stack(k), q) * SCALE
    parts = []
    for h in range(HEADS):
        one = s[h * L : (h + 1) * L]
        e = jnp.exp(one - jnp.max(one, axis=0, keepdims=True))
        parts.append((e * (1.0 / jnp.sum(e, axis=0, keepdims=True))).astype(BF16))
    return jnp.concatenate(parts, axis=0)


def attn_out(p, v):
    return dot_tn(p, head_stack(v)).astype(BF16)


def attn_back(p, q, k, v, do):
    dp = dot_nt(head_stack(v), do)
    parts = []
    for h in range(HEADS):
        w = p[h * L : (h + 1) * L].astype(F32)
        t = dp[h * L : (h + 1) * L]
        t = t - jnp.sum(t * w, axis=0, keepdims=True)
        parts.append((t * w * SCALE).astype(BF16))
    ds = jnp.concatenate(parts, axis=0)
    dq = dot_tn(ds, head_stack(k)).astype(BF16)
    dk = dot_nn(side_by_side(ds), head_stack(q)).astype(BF16)
    dv = dot_nn(side_by_side(p), head_stack(do)).astype(BF16)
    return jnp.concatenate([dq, dk, dv], axis=1)


def norm_back(v, c, dn, gain):
    u, inverse = norm_parts(v)
    du = dn * gain
    inner = jnp.mean(du * u, axis=-1, keepdims=True)
    dv = c + inverse * (du - u * inner)
    return dv, jnp.sum(u * dn, axis=0, keepdims=True)


def fused_kernel(
    scaling,
    x_ref, g_ref, ct_ref, gains_ref, rw_ref, cw_ref,
    gi_ref, gr_ref, gc_ref, gg_ref, ctx_ref,
    xbuf, ctin, flat, gsend, gcol, hsend, hrecv, cols, cots, ghsend, ghrecv,
    nbuf, obuf, qkvbuf, pbuf, dbuf, cbuf, gisend,
    wsend, wpair, wred, wside, wquart, wrecv, wfull, ctacc, ctpair, ctrecv, gacc, gpair, grecv, wr_ref, wc_ref,
    send_sem, recv_sem,
):
    band, block = lax.axis_index("band"), lax.axis_index("block")
    me = band * NB + block
    mycol = 2 * block + band

    def peer(i):
        other = lax.rem(me + i, ND)
        return other, other // NB, lax.rem(other, NB)

    def remote(phase, src, dst, to, frm, b, k):
        return pltpu.make_async_remote_copy(
            src_ref=src, dst_ref=dst, send_sem=send_sem.at[phase, to],
            recv_sem=recv_sem.at[phase, frm],
            device_id={"band": b, "block": k}, device_id_type=pl.DeviceIdType.MESH,
        )

    def every(fn, count):
        def step(i, _):
            fn(i)
            return 0
        lax.fori_loop(1, count, step, 0)

    def rows64(ref, j):
        return ref.at[pl.ds(pl.multiple_of(j * 64, 64), 64)]

    def rows8(ref, j):
        return ref.at[pl.ds(pl.multiple_of(j * 8, 8), 8)]

    barrier = pltpu.get_barrier_semaphore()

    def greet(i):
        _, b, k = peer(i)
        pl.semaphore_signal(
            barrier, inc=1, device_id={"band": b, "block": k},
            device_id_type=pl.DeviceIdType.MESH,
        )

    every(greet, ND)
    pl.semaphore_wait(barrier, ND - 1)

    def in_copy(t, to, frm):
        return remote(
            t, x_ref.at[pl.ds(to * 8 + t * GROUP, GROUP)],
            xbuf.at[pl.ds(t * GROUP, GROUP), pl.ds(pl.multiple_of(frm * 16, 16), 16)],
            to, frm, band, to,
        )

    def ct_copy(to, frm):
        return remote(4, ct_ref.at[to], ctin.at[frm], to, frm, band, to)

    def ring(i):
        return lax.rem(block + i, NB)

    def groups(fn, least=0, most=8 // GROUP):
        def step(t, _):
            fn(t)
            return 0
        lax.fori_loop(least, most, step, 0)

    groups(lambda t: every(lambda i: in_copy(t, ring(i), block).start(), NB))
    every(lambda i: ct_copy(ring(i), block).start(), NB)
    xbuf[:, pl.ds(pl.multiple_of(block * 16, 16), 16)] = x_ref[pl.ds(pl.multiple_of(block * 8, 8), 8)]
    ctin[block] = ct_ref[block]

    def spread(t, _):
        wide = g_ref[t].astype(F32)
        base = (t // 8) * 64 + lax.rem(t, 8)
        for half in range(2):
            for lo in range(2):
                flat[lo, pl.ds(base + half * 512, 8, stride=8), :] = wide[
                    half * 8 : half * 8 + 8, lo * L : lo * L + L
                ]
        return 0

    lax.fori_loop(0, 64, spread, 0)
    for lo in range(2):
        gsend[:, lo * L : lo * L + L] = flat[lo].astype(BF16)

    def half512(ref, j):
        return ref.at[pl.ds(pl.multiple_of(j * 512, 512), 512)]

    def g_copy(to, frm):
        return remote(5, half512(gsend, to), half512(gcol, frm), to, frm, to, block)

    other = 1 - band
    g_copy(other, band).start()
    gcol[pl.ds(pl.multiple_of(band * 512, 512), 512)] = gsend[pl.ds(pl.multiple_of(band * 512, 512), 512)]

    for m in range(3):
        wr_ref[:, m * D : (m + 1) * D] = rw_ref[m]
        wc_ref[:, m * D : (m + 1) * D] = cw_ref[m]

    gain_r = gains_ref[0:1, :]
    gain_c = gains_ref[1:2, :]
    span = GROUP * L

    def row_fwd(t, _):
        every(lambda i: in_copy(t, block, ring(i)).wait_recv(), NB)
        at = pl.ds(pl.multiple_of(t * span, span), span)
        v = jnp.concatenate([xbuf[t * GROUP + i] for i in range(GROUP)], axis=0).astype(F32)
        u, _inv = norm_parts(v)
        n = (u * gain_r).astype(BF16)
        qkv = dot_nn(n, wr_ref[...]).astype(BF16)
        outs = []
        for i in range(GROUP):
            own = qkv[i * L : (i + 1) * L]
            p = attn_probs(own[:, :D], own[:, D : 2 * D])
            pbuf[t * GROUP + i] = p
            outs.append(attn_out(p, own[:, 2 * D :]))
        o = jnp.concatenate(outs, axis=0)
        nbuf[at] = n
        obuf[at] = o
        qkvbuf[at] = qkv
        hidden = v + dot_nn(o, rw_ref[3])
        for i in range(GROUP):
            for lo in range(2):
                flat[lo, pl.ds(t * GROUP + i, L, stride=8), :] = hidden[
                    i * L : (i + 1) * L, lo * L : lo * L + L
                ]
        return 0

    lax.fori_loop(0, 8 // GROUP, row_fwd, 0)
    for lo in range(2):
        hsend[:, lo * L : lo * L + L] = flat[lo].astype(BF16)

    def part32(ref, j, u):
        return ref.at[pl.ds(pl.multiple_of(j * 64 + u * 32, 32), 32)]

    def h_send(u, i):
        o_, b, k = peer(i)
        return remote(6 + u, part32(hsend, 2 * k + b, u), part32(hrecv, me, u), o_, me, b, k)

    def h_recv(u, i):
        o_, b, k = peer(i)
        return remote(6 + u, part32(hsend, mycol, u), part32(hrecv, o_, u), o_, o_, b, k)

    groups(lambda u: every(lambda i: h_send(u, i).start(), ND), 0, 2)
    hrecv[pl.ds(pl.multiple_of(me * 64, 64), 64)] = hsend[pl.ds(pl.multiple_of(mycol * 64, 64), 64)]
    g_copy(band, other).wait_recv()
    cots[...] = gcol[...].astype(F32).reshape(ND, 8, 8, D)

    gacc[...] = jnp.zeros_like(gacc)

    def col_step(t, _):
        at = pl.ds(pl.multiple_of(1024 + t * span, span), span)
        v = jnp.concatenate([cols[:, t * GROUP + i].reshape(L, D) for i in range(GROUP)], axis=0)
        c = jnp.concatenate([cots[:, t * GROUP + i].reshape(L, D) for i in range(GROUP)], axis=0)
        cb = c.astype(BF16)
        u, _inv = norm_parts(v)
        n = (u * gain_c).astype(BF16)
        qkv = dot_nn(n, wc_ref[...]).astype(BF16)
        do = dot_nt(cb, cw_ref[3]).astype(BF16)
        outs, backs = [], []
        for i in range(GROUP):
            own = qkv[i * L : (i + 1) * L]
            q, k, w = own[:, :D], own[:, D : 2 * D], own[:, 2 * D :]
            p = attn_probs(q, k)
            outs.append(attn_out(p, w))
            backs.append(attn_back(p, q, k, w, do[i * L : (i + 1) * L]))
        dqkv = jnp.concatenate(backs, axis=0)
        nbuf[at] = n
        obuf[at] = jnp.concatenate(outs, axis=0)
        dbuf[at] = dqkv
        cbuf[at] = cb
        dn = dot_nt(dqkv, wc_ref[...])
        dv, ggain = norm_back(v, c, dn, gain_c)
        gacc[2:3, :] += ggain[:, :L]
        gacc[3:4, :] += ggain[:, L:]
        for i in range(GROUP):
            cols[:, t * GROUP + i] = dv[i * L : (i + 1) * L].reshape(ND, 8, D)
        return 0

    def gh_send(u, i):
        o_, b, k = peer(i)
        return remote(8 + u, part32(ghsend, o_, u), part32(ghrecv, mycol, u), o_, me, b, k)

    def gh_recv(u, i):
        o_, b, k = peer(i)
        return remote(8 + u, part32(ghsend, me, u), part32(ghrecv, 2 * k + b, u), o_, o_, b, k)

    def col_half(u):
        every(lambda i: h_recv(u, i).wait_recv(), ND)

        def take(j, _):
            at = pl.ds(pl.multiple_of(j * 64 + u * 32, 32), 32)
            cols[j, pl.ds(u * 4, 4)] = hrecv[at].astype(F32).reshape(4, 8, D)
            return 0

        lax.fori_loop(0, ND, take, 0)
        lax.fori_loop(u * (4 // GROUP), (u + 1) * (4 // GROUP), col_step, 0)

        def give(j, _):
            at = pl.ds(pl.multiple_of(j * 64 + u * 32, 32), 32)
            ghsend[at] = cols[j, pl.ds(u * 4, 4)].reshape(32, D).astype(BF16)
            return 0

        lax.fori_loop(0, ND, give, 0)
        every(lambda i: gh_send(u, i).start(), ND)

    groups(col_half, 0, 2)
    ghrecv[pl.ds(pl.multiple_of(mycol * 64, 64), 64)] = ghsend[pl.ds(pl.multiple_of(me * 64, 64), 64)]

    def weight_grads(start, slot):
        span_all = pl.ds(start, 1024)
        n = nbuf[span_all]
        for m in range(3):
            wsend[slot, m * D : (m + 1) * D] = (
                dot_tn(n, dbuf[span_all, m * D : (m + 1) * D]) * scaling
            ).astype(BF16)
        wsend[slot, 3 * D : 4 * D] = (dot_tn(obuf[span_all], cbuf[span_all]) * scaling).astype(BF16)

    def pair_copy(slot, to, frm):
        return remote(14 + slot, half512(wsend.at[slot], to), wpair.at[slot], to, frm, to, block)

    def back_copy(slot, to, frm):
        return remote(
            16 + slot, half512(wfull.at[slot], frm), half512(wfull.at[slot], frm), to, frm, to, block
        )

    near, far = lax.rem(block, 2), block // 2
    across = 2 * far + 1 - near
    quarter = pl.multiple_of(band * 512 + near * 256, 256)
    across_quarter = pl.multiple_of(band * 512 + (1 - near) * 256, 256)
    own_at = pl.multiple_of(band * 512 + near * 256 + far * 64, 64)
    NF = NB // 2

    def far_ring(i):
        return lax.rem(far + i, NF)

    def side_copy(slot, to, frm):
        return remote(
            26 + slot, wred.at[slot, pl.ds(pl.multiple_of((1 - near) * 256, 256), 256)],
            wside.at[slot], to, frm, band, to,
        )

    def side_back(slot, to, frm, at):
        part = wfull.at[slot, pl.ds(at, 256)]
        return remote(28 + slot, part, part, to, frm, band, to)

    def rs_copy(slot, to, frm):
        return remote(
            10 + slot, rows64(wquart.at[slot], to), wrecv.at[slot, frm], to, frm,
            band, 2 * to + near,
        )

    def ag_copy(slot, to, frm):
        at = pl.multiple_of(band * 512 + near * 256 + frm * 64, 64)
        own = wfull.at[slot, pl.ds(at, 64)]
        return remote(12 + slot, own, own, to, frm, band, 2 * to + near)

    def reduce_pair(slot):
        pair_copy(slot, band, other).wait_recv()
        own = wsend[slot, pl.ds(pl.multiple_of(band * 512, 512), 512)].astype(F32)
        wred[slot] = (own + wpair[slot].astype(F32)).astype(BF16)
        side_copy(slot, across, block).start()

    def reduce_side(slot):
        side_copy(slot, block, across).wait_recv()
        own = wred[slot, pl.ds(pl.multiple_of(near * 256, 256), 256)].astype(F32)
        wquart[slot] = (own + wside[slot].astype(F32)).astype(BF16)
        every(lambda i: rs_copy(slot, far_ring(i), far).start(), NF)

    def reduce_own(slot):
        wrecv[slot, far] = wquart[slot, pl.ds(pl.multiple_of(far * 64, 64), 64)]
        every(lambda i: rs_copy(slot, far, far_ring(i)).wait_recv(), NF)
        total = wrecv[slot, 0].astype(F32)
        for j in range(1, NF):
            total = total + wrecv[slot, j].astype(F32)
        wfull[slot, pl.ds(own_at, 64)] = total.astype(BF16)
        every(lambda i: ag_copy(slot, far_ring(i), far).start(), NF)

    def gather_side(slot):
        every(lambda i: ag_copy(slot, far, far_ring(i)).wait_recv(), NF)
        side_back(slot, across, block, quarter).start()

    def gather_back(slot):
        side_back(slot, block, across, across_quarter).wait_recv()
        back_copy(slot, other, band).start()

    weight_grads(1024, 1)
    pair_copy(1, other, band).start()

    every(lambda i: ct_copy(block, ring(i)).wait_recv(), NB)
    tiles = ctin[0]
    for j in range(1, NB):
        tiles = tiles + ctin[j]
    tile_ids = tiles.astype(jnp.int32)
    ctin[0] = tile_ids.astype(F32)

    groups(lambda u: every(lambda i: gh_recv(u, i).wait_recv(), ND), 0, 2)
    reduce_pair(1)
    for lo in range(2):
        flat[lo] = ghrecv[:, lo * L : lo * L + L].astype(F32)

    ctacc[...] = jnp.zeros_like(ctacc)

    def gi_copy(t, to, frm):
        return remote(
            18 + t,
            gisend.at[pl.ds(t * GROUP, GROUP), pl.ds(pl.multiple_of(to * 16, 16), 16)],
            gi_ref.at[pl.ds(frm * 8 + t * GROUP, GROUP)], to, frm, band, to,
        )

    def row_bwd(t, _):
        at = pl.ds(pl.multiple_of(t * span, span), span)
        v = jnp.concatenate([xbuf[t * GROUP + i] for i in range(GROUP)], axis=0).astype(F32)
        c = jnp.concatenate(
            [
                jnp.concatenate(
                    [flat[lo, pl.ds(t * GROUP + i, L, stride=8), :] for lo in range(2)], axis=1
                )
                for i in range(GROUP)
            ],
            axis=0,
        )
        cb = c.astype(BF16)
        do = dot_nt(cb, rw_ref[3]).astype(BF16)
        qkv = qkvbuf[at]
        backs = []
        for i in range(GROUP):
            own = qkv[i * L : (i + 1) * L]
            backs.append(
                attn_back(
                    pbuf[t * GROUP + i], own[:, :D], own[:, D : 2 * D], own[:, 2 * D :],
                    do[i * L : (i + 1) * L],
                )
            )
        dqkv = jnp.concatenate(backs, axis=0)
        dbuf[at] = dqkv
        cbuf[at] = cb
        dn = dot_nt(dqkv, wr_ref[...])
        dv, ggain = norm_back(v, c, dn, gain_r)
        gacc[0:1, :] += ggain[:, :L]
        gacc[1:2, :] += ggain[:, L:]
        dvb = dv.astype(BF16)
        which = ctin[0, pl.ds((t * GROUP) // 4, 1), :]
        rows_of = lax.broadcasted_iota(jnp.int32, (CT, L), 0).astype(F32)
        hot = jnp.where(rows_of == which, 1.0, 0.0).astype(BF16)
        for i in range(GROUP):
            gisend[t * GROUP + i] = dvb[i * L : (i + 1) * L]
            ctacc[...] += dot_nn(hot, dvb[i * L : (i + 1) * L])
        every(lambda i: gi_copy(t, ring(i), block).start(), NB)

        @pl.when(t == 1)
        def _():
            reduce_side(1)

        return 0

    lax.fori_loop(0, 8 // GROUP, row_bwd, 0)

    weight_grads(0, 0)
    pair_copy(0, other, band).start()

    def half64(ref, j):
        return ref.at[pl.ds(pl.multiple_of(j * 64, 64), 64)]

    def cx_pair(to, frm):
        return remote(24, half64(ctacc, to), ctpair, to, frm, to, block)

    def cx_copy(to, frm):
        return remote(22, rows8(ctacc, band * NB + to), ctrecv.at[frm], to, frm, band, to)

    def gg_pair(to, frm):
        return remote(25, gacc, gpair, to, frm, to, block)

    def gg_copy(to, frm):
        return remote(23, gpair, grecv.at[frm], to, frm, band, to)

    cx_pair(other, band).start()
    gg_pair(other, band).start()
    reduce_pair(0)
    reduce_own(1)
    reduce_side(0)
    gi_ref[pl.ds(pl.multiple_of(block * 8, 8), 8)] = gisend[:, pl.ds(pl.multiple_of(block * 16, 16), 16)]
    cx_pair(band, other).wait_recv()
    mine64 = pl.ds(pl.multiple_of(band * 64, 64), 64)
    ctacc[mine64] = ctacc[mine64] + ctpair[...]
    gg_pair(band, other).wait_recv()
    gpair[...] = gpair[...] + gacc[...]
    every(lambda i: cx_copy(ring(i), block).start(), NB)
    every(lambda i: gg_copy(ring(i), block).start(), NB)
    ctrecv[block] = ctacc[pl.ds(pl.multiple_of(me * 8, 8), 8)]
    grecv[block] = gpair[...]
    gather_side(1)
    reduce_own(0)
    gather_back(1)
    gather_side(0)
    every(lambda i: cx_copy(block, ring(i)).wait_recv(), NB)
    every(lambda i: gg_copy(block, ring(i)).wait_recv(), NB)
    total, gtotal = ctrecv[0], grecv[0]
    for j in range(1, NB):
        total = total + ctrecv[j]
        gtotal = gtotal + grecv[j]
    ctx_ref[...] = 0.25 * total
    gtotal = gtotal * scaling
    for m in range(2):
        gg_ref[m : m + 1, :] = jnp.concatenate([gtotal[2 * m : 2 * m + 1], gtotal[2 * m + 1 : 2 * m + 2]], axis=1)
    back_copy(1, band, other).wait_recv()
    gc_ref[...] = wfull[1].astype(F32).reshape(4, D, D)
    gather_back(0)
    groups(lambda t: every(lambda i: gi_copy(t, block, ring(i)).wait_recv(), NB))
    back_copy(0, band, other).wait_recv()
    gr_ref[...] = wfull[0].astype(F32).reshape(4, D, D)

    groups(lambda t: every(lambda i: in_copy(t, ring(i), block).wait_send(), NB))
    every(lambda i: ct_copy(ring(i), block).wait_send(), NB)
    g_copy(other, band).wait_send()
    groups(lambda u: every(lambda i: h_send(u, i).wait_send(), ND), 0, 2)
    groups(lambda u: every(lambda i: gh_send(u, i).wait_send(), ND), 0, 2)
    for slot in range(2):
        pair_copy(slot, other, band).wait_send()
        back_copy(slot, other, band).wait_send()
        side_copy(slot, across, block).wait_send()
        side_back(slot, across, block, quarter).wait_send()
        every(lambda i: rs_copy(slot, far_ring(i), far).wait_send(), NF)
        every(lambda i: ag_copy(slot, far_ring(i), far).wait_send(), NF)
    groups(lambda t: every(lambda i: gi_copy(t, ring(i), block).wait_send(), NB))
    cx_pair(other, band).wait_send()
    gg_pair(other, band).wait_send()
    every(lambda i: cx_copy(ring(i), block).wait_send(), NB)
    every(lambda i: gg_copy(ring(i), block).wait_send(), NB)


def fused_shards(grid_input, grad_output, context_tile, gains, row_weights, column_weights):
    cell_count = grid_input.shape[0] * grid_input.shape[1] * ND
    scaling = 1.0 / math.sqrt(cell_count)
    block = lax.axis_index("block")
    cells = jnp.repeat(context_tile.astype(F32), 4, axis=1).reshape(NB, 2, 16)
    lanes = jnp.tile(cells, (1, 1, NB))
    mine = (lax.iota(jnp.int32, L) // 16) == block
    placed = jnp.pad(jnp.where(mine, lanes, 0.0), ((0, 0), (0, 6), (0, 0)))
    vm = pl.BlockSpec(memory_space=pltpu.VMEM)
    big = lambda n, d=D, t=BF16: pltpu.VMEM((n, d), t)
    outs = pl.pallas_call(
        functools.partial(fused_kernel, scaling),
        out_shape=(
            jax.ShapeDtypeStruct((64, 16, D), BF16),
            jax.ShapeDtypeStruct((4, D, D), F32),
            jax.ShapeDtypeStruct((4, D, D), F32),
            jax.ShapeDtypeStruct((2, D), F32),
            jax.ShapeDtypeStruct((TILE_DEV, D), F32),
        ),
        in_specs=[vm] * 6,
        out_specs=(vm,) * 5,
        scratch_shapes=[
            pltpu.VMEM((8, L, D), BF16),
            pltpu.VMEM((NB, 8, L), F32),
            pltpu.VMEM((2, 1024, L), F32),
            big(1024), big(1024), big(1024), big(1024),
            pltpu.VMEM((ND, 8, 8, D), F32),
            pltpu.VMEM((ND, 8, 8, D), F32),
            big(1024), big(1024),
            big(2048), big(2048), big(1024, 3 * D),
            pltpu.VMEM((8, HEADS * L, L), BF16),
            big(2048, 3 * D), big(2048),
            pltpu.VMEM((8, L, D), BF16),
            pltpu.VMEM((2, 1024, D), BF16),
            pltpu.VMEM((2, 512, D), BF16),
            pltpu.VMEM((2, 512, D), BF16),
            pltpu.VMEM((2, 256, D), BF16),
            pltpu.VMEM((2, 256, D), BF16),
            pltpu.VMEM((2, NB // 2, 64, D), BF16),
            pltpu.VMEM((2, 1024, D), BF16),
            big(CT, D, F32),
            big(64, D, F32),
            pltpu.VMEM((NB, TILE_DEV, D), F32),
            big(8, L, F32),
            big(8, L, F32),
            pltpu.VMEM((NB, 8, L), F32),
            big(D, 3 * D), big(D, 3 * D),
            pltpu.SemaphoreType.DMA((30, ND)),
            pltpu.SemaphoreType.DMA((30, ND)),
        ],
        compiler_params=pltpu.CompilerParams(
            collective_id=0, has_side_effects=True, vmem_limit_bytes=56 * 1024 * 1024
        ),
    )(grid_input, grad_output, placed, gains, row_weights, column_weights)
    return outs


def solution(mesh):
    in_specs = (
        P(("parts", "band"), "block", None),
        P(("parts", "band"), "block", None),
        P(("parts", "band"), "block"),
        P(),
        P(),
        P(),
    )
    out_specs = (
        P(("parts", "band"), "block", None),
        P("parts", None, None),
        P("parts", None, None),
        P("parts", None),
        P(("parts", "band", "block"), None),
    )
    chosen = fused_shards if fits_fused(mesh) else shards
    return jax.shard_map(chosen, mesh=mesh, in_specs=in_specs, out_specs=out_specs, check_vma=False)
```
